32 devices in a mesh: seg: 8 (over z, x), blk: 4 (over y, core).
Axes of the slice: x: 2, y: 2, z: 4, core: 2. Of those that a mesh axis runs over, the one named last changes fastest.
Arguments:
- tokens: bfloat16 [32, 2048, 768], P('seg', 'blk'), may hold values from -6 to 6
- memory: bfloat16 [32, 256, 768], P('seg'), may hold values from -6 to 6
- present: int32 [32], P('seg'), may hold values 0 or 1
- block_pos: int32 [32, 4], P('seg'), may hold values from 0 to 3, each once within a row
- ln1_gain: float32 [768], replicated, may hold values from 0.5 to 1.5
- ln1_bias: float32 [768], replicated, may hold values from -4 to 4
- w_qkv: bfloat16 [768, 2304], replicated, may hold values from -0.3125 to 0.3125
- w_out: bfloat16 [768, 768], replicated, may hold values from -0.4375 to 0.4375
- ln2_gain: float32 [768], replicated, may hold values from 0.5 to 1.5
- ln2_bias: float32 [768], replicated, may hold values from -4 to 4
- w_fc: bfloat16 [768, 3072], replicated, may hold values from -0.21875 to 0.21875
- w_proj: bfloat16 [3072, 768], replicated, may hold values from -0.15625 to 0.15625
- w_mu: float32 [12, 256], replicated, may hold values from -0.25 to 0.25
- w_sig: float32 [12, 256], replicated, may hold values from -0.25 to 0.25
- grad_out: bfloat16 [32, 2048, 768], P('seg', 'blk'), may hold values from -6 to 6
- grad_memory: bfloat16 [32, 256, 768], P('seg'), may hold values from -6 to 6
Outputs:
- result: bfloat16 [32, 2048, 768], P('seg', 'blk')
- new_memory: bfloat16 [32, 256, 768], P('seg')
- grad_tokens: bfloat16 [32, 2048, 768], P('seg', 'blk')
- memory_grad: bfloat16 [32, 256, 768], P('seg')
- ln1_gain_grad: float32 [768], replicated
- ln1_bias_grad: float32 [768], replicated
- w_qkv_grad: float32 [768, 2304], replicated
- w_out_grad: float32 [768, 768], replicated
- ln2_gain_grad: float32 [768], replicated
- ln2_bias_grad: float32 [768], replicated
- w_fc_grad: float32 [768, 3072], replicated
- w_proj_grad: float32 [3072, 768], replicated
- w_mu_grad: float32 [12, 256], replicated
- w_sig_grad: float32 [12, 256], replicated
The draws below stay inside these ranges and needn't reach their ends.
Inputs may be any that keep to these rules, and one draw needn't show every extreme that they name: `present`: 1 where a segment carries memory, 0 where it starts empty. Each row is a permutation; index i of blk holds the 512 consecutive positions of block block_pos[s, i] of segment s.
All inputs are finite; a program needn't handle non-finite values. No bound on the sum of `present` on one device may be relied on, other than what follows from the above.
Results may differ from the reference program's by a relative error of at most 0.03.
The reference program's roundings to bfloat16 on the way count: a program that leaves them out, or rounds other values in their place, can miss the bound.
Values may be sent and summed in bfloat16 or wider, within the bound.
No kernel may reach another device: no remote copies, remote signals or barrier semaphores. Data moves between devices by JAX's collectives and lax.ppermute only.
A program may use at most 384 MiB of HBM per device.

```python
import jax
import jax.numpy as jnp
from jax import lax

D = 768
H = 12
HD = 64
FF = 3072
NB = 256
SEG_LEN = 2048
SEGS = 32
N_BLK = 4


def place_ends(values, rng, least, largest):
    spot = [jax.random.randint(jax.random.fold_in(rng, axis), (), 0, length) for axis, length in enumerate(values.shape)]
    main_axis = values.shape.index(max(values.shape))
    neighbour = spot[:main_axis] + [(spot[main_axis] + 1) % values.shape[main_axis]] + spot[main_axis + 1:]
    return values.at[tuple(spot)].set(least).at[tuple(neighbour)].set(largest)


def with_spikes(values, stream_key, source, target, shards_of, factor):
    owner, partner = [(jnp.arange(values.shape[dim]) // (values.shape[dim] // shards_of)).reshape([-1 if axis == dim else 1 for axis in range(values.ndim)]) for dim in (source, target)]
    chosen = jax.random.permutation(stream_key, shards_of)[partner]
    strong = (owner == chosen) | (owner == (partner + shards_of // 2) % shards_of)
    return jnp.where(strong, factor * values, values)


def shard_levels(stream_key, shape, cuts, least, largest):
    def one(dim, parts):
        heights = jax.random.uniform(jax.random.fold_in(jax.random.fold_in(stream_key, 6), dim), (parts,), jnp.float32, least / len(cuts), largest / len(cuts))
        return jnp.repeat(jnp.exp(heights), shape[dim] // parts).reshape((-1,) + (1,) * (len(shape) - dim - 1))

    loudness = one(*cuts[0])
    for cut in cuts[1:]:
        loudness = loudness * one(*cut)
    return loudness


def scatter_about(stream_key, extent, deviation, bound, cuts=(), kind=jnp.bfloat16):
    array = jax.random.normal(stream_key, extent, jnp.float32) * deviation
    if len(cuts) > 0:
        array = shard_levels(stream_key, extent, cuts, -0.22, 0.18) * array
    return jnp.clip(array, min=-bound, max=bound).astype(kind)


def gaussian_with(rng, dims, spread, limit, shards, heavy, kind=jnp.bfloat16):
    values = spread * jax.random.normal(rng, dims, jnp.float32)
    if shards:
        values = values * shard_levels(rng, dims, shards, -0.22, 0.18)
    return jnp.clip(with_spikes(values, jax.random.fold_in(rng, 3), *heavy), -limit, limit).astype(kind)


def setup_inputs(seed: int = 0) -> dict:
    streams_of = jax.random.split(jax.random.key(seed), 17)
    return {
        "tokens": gaussian_with(streams_of[0], (SEGS, SEG_LEN, D), 1.0, 6.0, ((0, 8), (1, 4)), (1, 2, 4, 2.0)),
        "memory": scatter_about(streams_of[1], (SEGS, NB, D), 1.0, 6.0, ((0, 8),)),
        "present": place_ends((jax.random.randint(streams_of[2], (SEGS,), 0, 2) < 1).astype(jnp.int32), jax.random.fold_in(streams_of[2], 1), 0, 1),
        "block_pos": jax.vmap(lambda own: jax.random.permutation(own, N_BLK))(jax.random.split(streams_of[3], SEGS)).reshape((SEGS, N_BLK)).astype(jnp.int32),
        "ln1_gain": jnp.clip(1.0 + 0.1 * jax.random.normal(streams_of[4], (D,), jnp.float32), 0.5, 1.5),
        "ln1_bias": scatter_about(streams_of[5], (D,), 0.3, 4.0, (), jnp.float32),
        "w_qkv": scatter_about(streams_of[6], (D, 3 * D), (D // 2) ** -0.5, 0.3125),
        "w_out": scatter_about(streams_of[7], (D, D), (D // 4) ** -0.5, 0.4375),
        "ln2_gain": jnp.clip(1.0 + 0.1 * jax.random.normal(streams_of[8], (D,), jnp.float32), 0.5, 1.5),
        "ln2_bias": scatter_about(streams_of[9], (D,), 0.3, 4.0, (), jnp.float32),
        "w_fc": scatter_about(streams_of[10], (D, FF), D ** -0.5, 0.21875),
        "w_proj": scatter_about(streams_of[11], (FF, D), (FF // 2) ** -0.5, 0.15625),
        "w_mu": scatter_about(streams_of[12], (H, NB), (2 * NB) ** -0.5, 0.25, (), jnp.float32),
        "w_sig": scatter_about(streams_of[13], (H, NB), (2 * NB) ** -0.5, 0.25, (), jnp.float32),
        "grad_out": gaussian_with(streams_of[14], (SEGS, SEG_LEN, D), 1.0, 6.0, ((0, 8), (1, 4)), (0, 2, 8, 2.0)),
        "grad_memory": scatter_about(streams_of[15], (SEGS, NB, D), 1.0, 6.0, ((0, 8),)),
    }


eps_norm = 1e-05
ridge_weight = 1.0
contract = 0.5
spread_var = 0.05
spread_floor = 0.002
masked_value = -1e+30
highest = lax.Precision.HIGHEST

@jax.custom_vjp
def low(v):
    return lax.optimization_barrier(v.astype(jnp.bfloat16)).astype(jnp.float32)

@jax.custom_vjp
def low_back(v):
    return v

def low_keep(v):
    return (low(v), None)

def low_pass(kept, grad):
    return (grad,)

def back_keep(v):
    return (v, None)

def back_low(kept, grad):
    return (low(grad),)
low.defvjp(low_keep, low_pass)
low_back.defvjp(back_keep, back_low)

def layer_norm(values, gain_vec, shift_vec):
    centred = values - lax.optimization_barrier(jnp.mean(values, axis=-1, keepdims=True))
    inverse = lax.rsqrt(lax.optimization_barrier(jnp.mean(centred * centred, axis=-1, keepdims=True)) + eps_norm)
    return centred * inverse * gain_vec + shift_vec

def basis_table(points, basis_count):
    centres = (jnp.arange(basis_count, dtype=jnp.float32) + 0.5) / basis_count
    width_b = 0.75 / basis_count
    offset = points[..., None] - centres
    return jnp.exp(-offset * offset / (2.0 * width_b * width_b))

def token_times(positions, seg_len):
    return contract + (1.0 - contract) * (positions.astype(jnp.float32) + 0.5) / seg_len

def memory_tables(basis_count, seg_len):
    samples = (jnp.arange(basis_count, dtype=jnp.float32) + 0.5) / basis_count
    squeezed = basis_table(contract * samples, basis_count)
    stretched = basis_table(samples, basis_count)
    carry_map = jnp.dot(squeezed.T, stretched, precision=highest)
    all_times = basis_table(token_times(jnp.arange(seg_len, dtype=jnp.int32), seg_len), basis_count)
    gram_matrix = jnp.dot(squeezed.T, squeezed, precision=highest) + jnp.dot(all_times.T, all_times, precision=highest)
    gram_matrix = gram_matrix + ridge_weight * jnp.eye(basis_count, dtype=jnp.float32)
    return (carry_map, jnp.linalg.cholesky(gram_matrix))

def memory_density(mem_scores, w_mu, w_sig):
    basis_count = w_mu.shape[-1]
    centres = (jnp.arange(basis_count, dtype=jnp.float32) + 0.5) / basis_count
    width_b = 0.75 / basis_count
    centre_arg = lax.optimization_barrier(jnp.sum(mem_scores * w_mu, axis=-1))
    spread_arg = lax.optimization_barrier(jnp.sum(mem_scores * w_sig, axis=-1))
    centre = jax.nn.sigmoid(centre_arg)
    spread_total = spread_var * jax.nn.softplus(spread_arg) + spread_floor
    offset = centre[..., None] - centres
    return width_b * lax.rsqrt(spread_total)[..., None] * jnp.exp(-offset * offset / (2.0 * spread_total[..., None]))

def segment_forward(params, tok_seg, mem_seg, memory_on, block_order, tables):
    ln1_gain, ln1_bias, w_qkv, w_out, ln2_gain, ln2_bias, w_fc, w_proj, w_mu, w_sig = params
    carry_map, factor = tables
    block_rows = SEG_LEN // N_BLK
    local_pos = jnp.arange(SEG_LEN, dtype=jnp.int32)
    positions = block_order[local_pos // block_rows].astype(jnp.int32) * block_rows + local_pos % block_rows
    normed_low = low(layer_norm(tok_seg, ln1_gain, ln1_bias))
    projected = low(low_back(jnp.dot(normed_low, w_qkv, precision=highest)))
    queries = projected[:, :D].reshape(SEG_LEN, H, HD)
    keys_tok = projected[:, D:2 * D].reshape(SEG_LEN, H, HD)
    values_tok = projected[:, 2 * D:].reshape(SEG_LEN, H, HD)
    mem_keys = low(low_back(jnp.dot(mem_seg, w_qkv[:, D:2 * D], precision=highest))).reshape(NB, H, HD)
    mem_values = low(low_back(jnp.dot(mem_seg, w_qkv[:, 2 * D:], precision=highest))).reshape(NB, H, HD)
    score_scale = HD ** (-0.5)
    row_block = 512 if SEG_LEN % 512 == 0 else SEG_LEN

    def block_context(inputs):
        query_blk, pos_blk = inputs
        raw_scores = jnp.einsum('qhd,khd->hqk', query_blk, keys_tok, precision=highest) * score_scale
        allowed = pos_blk[:, None] >= positions[None, :]
        scores = jnp.where(allowed[None], low_back(raw_scores), masked_value)
        row_max = lax.optimization_barrier(jnp.max(scores, axis=-1, keepdims=True))
        exponent = jnp.exp(scores - row_max)
        attention_probs = exponent / lax.optimization_barrier(jnp.sum(exponent, axis=-1, keepdims=True))
        local_context = jnp.einsum('hqk,khd->qhd', low(attention_probs), values_tok, precision=highest)
        mem_scores = low_back(jnp.einsum('qhd,nhd->qhn', query_blk, mem_keys, precision=highest) * score_scale)
        density = low(memory_density(mem_scores, w_mu, w_sig))
        mem_context = jnp.einsum('qhn,nhd->qhd', density, mem_values, precision=highest)
        return local_context + memory_on * mem_context
    query_blocks = queries.reshape(SEG_LEN // row_block, row_block, H, HD)
    pos_blocks = positions.reshape(SEG_LEN // row_block, row_block)
    context = lax.map(jax.checkpoint(block_context), (query_blocks, pos_blocks)).reshape(SEG_LEN, D)
    attended = low(low_back(context))
    branch = low_back(jnp.dot(attended, w_out, precision=highest))
    middle = tok_seg + branch
    second = low(layer_norm(middle, ln2_gain, ln2_bias))
    hidden_pre = low_back(jnp.dot(second, w_fc, precision=highest))
    hidden = low(jax.nn.gelu(hidden_pre, approximate=True))
    mlp_out = low_back(jnp.dot(hidden, w_proj, precision=highest))
    result = middle + mlp_out
    basis_rows = basis_table(token_times(positions, SEG_LEN), NB)
    ridge_rhs = memory_on * jnp.dot(carry_map, mem_seg, precision=highest) + jnp.dot(basis_rows.T, normed_low, precision=highest)
    new_memory = jax.scipy.linalg.cho_solve((factor, True), ridge_rhs)
    return (result, new_memory)

def reference(tokens, memory, present, block_pos, ln1_gain, ln1_bias, w_qkv, w_out, ln2_gain, ln2_bias, w_fc, w_proj, w_mu, w_sig, grad_out, grad_memory):
    params = (ln1_gain.astype(jnp.float32), ln1_bias.astype(jnp.float32), w_qkv.astype(jnp.float32), w_out.astype(jnp.float32), ln2_gain.astype(jnp.float32), ln2_bias.astype(jnp.float32), w_fc.astype(jnp.float32), w_proj.astype(jnp.float32), w_mu.astype(jnp.float32), w_sig.astype(jnp.float32))
    tables = memory_tables(NB, SEG_LEN)

    def per_segment(totals, inputs):
        tok_seg, mem_seg, present_seg, order_seg, cot_seg, cot_mem = inputs
        memory_on = present_seg.astype(jnp.float32)

        def forward(params_now, tok_now, mem_now):
            return segment_forward(params_now, tok_now, mem_now, memory_on, order_seg, tables)
        outputs, pullback = jax.vjp(forward, params, tok_seg.astype(jnp.float32), mem_seg.astype(jnp.float32))
        grad_params, grad_tok, grad_mem = pullback((cot_seg.astype(jnp.float32), cot_mem.astype(jnp.float32)))
        totals = jax.tree.map(jnp.add, totals, grad_params)
        return (totals, (outputs[0].astype(jnp.bfloat16), outputs[1].astype(jnp.bfloat16), grad_tok.astype(jnp.bfloat16), grad_mem.astype(jnp.bfloat16)))
    zero_grads = jax.tree.map(jnp.zeros_like, params)
    totals, stacked = lax.scan(per_segment, zero_grads, (tokens, memory, present, block_pos, grad_out, grad_memory))
    return (stacked[0], stacked[1], stacked[2], stacked[3], totals[0], totals[1], totals[2], totals[3], totals[4], totals[5], totals[6], totals[7], totals[8], totals[9])
```

```python
from functools import partial
import math

import jax
import jax.numpy as jnp
import ml_dtypes
import numpy as np
from jax import lax
from jax.experimental import pallas as pl
from jax.experimental.pallas import tpu as pltpu
from jax.sharding import PartitionSpec as P

eps_norm = 1e-05
ridge_weight = 1.0
contract = 0.5
spread_var = 0.05
spread_floor = 0.002
masked_value = -1e30
LANES = 128
f32 = jnp.float32
bf16 = jnp.bfloat16

NN = (((1,), (0,)), ((), ()))
NT = (((1,), (1,)), ((), ()))
TN = (((0,), (0,)), ((), ()))


def mm(a, b, dims=NN):
    return lax.dot_general(a, b, dims, preferred_element_type=f32)


def basis_table(points, basis_count):
    centres = (np.arange(basis_count, dtype=np.float64) + 0.5) / basis_count
    width_b = 0.75 / basis_count
    offset = points[..., None] - centres
    return np.exp(-offset * offset / (2.0 * width_b * width_b))


def split_low(table):
    high_part = table.astype(ml_dtypes.bfloat16)
    low_part = (table - high_part.astype(np.float64)).astype(ml_dtypes.bfloat16)
    return high_part, low_part


def memory_tables(basis_count, seg_len):
    samples = (np.arange(basis_count, dtype=np.float64) + 0.5) / basis_count
    squeezed = basis_table(contract * samples, basis_count)
    stretched = basis_table(samples, basis_count)
    carry_map = squeezed.T @ stretched
    times = contract + (1.0 - contract) * (np.arange(seg_len, dtype=np.float64) + 0.5) / seg_len
    all_times = basis_table(times, basis_count)
    gram = squeezed.T @ squeezed + all_times.T @ all_times + ridge_weight * np.eye(basis_count)
    return np.linalg.solve(gram, all_times.T), np.linalg.solve(gram, carry_map)


def digit_route(size, stride, radix, distance):
    route = []
    for i in range(size):
        digit = (i // stride) % radix
        route.append((i, i + ((digit + distance) % radix - digit) * stride))
    return route


def pick(stack, index):
    return lax.dynamic_index_in_dim(stack, index, 0, keepdims=False)


def put(stack, block, index):
    return lax.dynamic_update_index_in_dim(stack, block, index, 0)


def scatter_step(parts, axis, stride, radix):
    if radix == 1:
        return parts[0]
    size = lax.axis_size(axis)
    digit = (lax.axis_index(axis) // stride) % radix
    total = pick(parts, digit).astype(f32)
    for distance in range(1, radix):
        sent = pick(parts, (digit + distance) % radix)
        total = total + lax.ppermute(sent, axis, digit_route(size, stride, radix, distance)).astype(f32)
    return total.astype(bf16)


def sum_step(block, axis, stride, radix):
    size = lax.axis_size(axis)
    total = block.astype(f32)
    for distance in range(1, radix):
        total = total + lax.ppermute(block, axis, digit_route(size, stride, radix, distance)).astype(f32)
    return total.astype(block.dtype)


def gather_step(block, axis, stride, radix):
    size = lax.axis_size(axis)
    digit = (lax.axis_index(axis) // stride) % radix
    if radix == 1:
        return block[None]
    stack = jnp.zeros((radix,) + block.shape, block.dtype)
    stack = put(stack, block, digit)
    for distance in range(1, radix):
        got = lax.ppermute(block, axis, digit_route(size, stride, radix, distance))
        stack = put(stack, got, (digit - distance) % radix)
    return stack


def near(size):
    return 2 if size % 2 == 0 else 1


def sum_weight(partial_grad):
    rows, columns = partial_grad.shape
    blk, seg = lax.axis_size("blk"), lax.axis_size("seg")
    core, side = near(blk), near(seg)
    block = partial_grad.astype(bf16)
    block = scatter_step(block.reshape(core, rows // core, columns), "blk", 1, core)
    rows = rows // core
    block = scatter_step(block.reshape(side, rows // side, columns), "seg", 1, side)
    rows, rest = rows // side, seg // side
    block = scatter_step(block.reshape(rest, rows // rest, columns), "seg", side, rest)
    block = sum_step(block, "blk", core, blk // core)
    block = gather_step(block, "seg", side, rest).reshape(rows, columns)
    block = gather_step(block, "seg", 1, side).reshape(rows * side, columns)
    block = gather_step(block, "blk", 1, core).reshape(rows * side * core, columns)
    return block.astype(f32)


def collect_blocks(stack, members):
    size = lax.axis_size("blk")
    member = lax.axis_index("blk") % members
    slots = [pick(stack, member)]
    for distance in range(1, members):
        sent = pick(stack, (member + distance) % members)
        slots.append(lax.ppermute(sent, "blk", digit_route(size, 1, members, distance)))
    return slots


def return_blocks(slots, members):
    size = lax.axis_size("blk")
    member = lax.axis_index("blk") % members
    stack = jnp.zeros((members,) + slots[0].shape, slots[0].dtype)
    stack = put(stack, slots[0], member)
    for distance in range(1, members):
        got = lax.ppermute(slots[distance], "blk", digit_route(size, 1, members, members - distance))
        stack = put(stack, got, (member + distance) % members)
    return stack


def share_segments(block, members):
    size = members
    if members % 2 == 0:
        stack = gather_step(block, "blk", 2, members // 2)
        stack = gather_step(stack, "blk", 1, 2)
        return jnp.swapaxes(stack, 0, 1).reshape((size,) + block.shape)
    return gather_step(block, "blk", 1, members)


def norm_rows(values, gain_vec, shift_vec):
    centred = values - jnp.mean(values, axis=-1, keepdims=True)
    inverse = lax.rsqrt(jnp.mean(centred * centred, axis=-1, keepdims=True) + eps_norm)
    unit_rows = centred * inverse
    return (unit_rows * gain_vec + shift_vec, unit_rows, inverse)


def norm_back(upstream, unit_rows, inverse, gain_vec):
    scaled = upstream * gain_vec
    back_part = inverse * (
        scaled
        - jnp.mean(scaled, axis=-1, keepdims=True)
        - unit_rows * jnp.mean(scaled * unit_rows, axis=-1, keepdims=True)
    )
    return (back_part, jnp.sum(upstream * unit_rows, axis=0), jnp.sum(upstream, axis=0))


def spread_parts(centre_arg, spread_arg):
    centre = 1.0 / (1.0 + jnp.exp(-centre_arg))
    tail = jnp.exp(-jnp.abs(spread_arg))
    spread = spread_var * (jnp.maximum(spread_arg, 0.0) + jnp.log(1.0 + tail)) + spread_floor
    return centre, spread


def forward_kernel(
    order, flag, q_ref, k_ref, v_ref, mv_ref, u_ref, att_ref, loc_ref, lse_ref, *, rows, count, head, scale
):
    lane = lax.broadcasted_iota(jnp.int32, (1, LANES), 1)
    inside = [lane // head == a for a in range(2)]
    sel = [jnp.where(m, 1.0, 0.0).astype(bf16) for m in inside]
    sel_scale = [jnp.where(m, scale, 0.0).astype(bf16) for m in inside]
    rest = [jnp.where(m, 0.0, 1.0).astype(bf16) for m in inside]
    basis = mv_ref.shape[0]
    centres = (lax.broadcasted_iota(jnp.int32, (1, basis), 1).astype(f32) + 0.5) / basis
    width_b = 0.75 / basis
    on = flag[0].astype(f32)
    ahead = lax.broadcasted_iota(jnp.int32, (rows, rows), 0) >= lax.broadcasted_iota(
        jnp.int32, (rows, rows), 1
    )

    def tile(j, carry, qs, diagonal):
        at = pl.multiple_of(order[j] * rows, rows)
        k = k_ref[pl.ds(at, rows), :]
        v = v_ref[pl.ds(at, rows), :]
        out = []
        for a in range(2):
            top, acc = carry[2 * a], carry[2 * a + 1]
            s = mm(qs[a], k, NT)
            if diagonal:
                s = jnp.where(ahead, s, masked_value)
            new_top = jnp.maximum(top, jnp.max(s, axis=1, keepdims=True))
            p = jnp.exp(s - new_top)
            acc = acc * jnp.exp(top - new_top) + mm(p.astype(bf16), v * sel[a] + rest[a])
            out += [new_top, acc]
        return tuple(out)

    def q_step(i, _):
        at = pl.multiple_of(order[i] * rows, rows)
        q = q_ref[pl.ds(at, rows), :]
        qs = [q * s for s in sel_scale]
        start = (jnp.full((rows, 1), masked_value, f32), jnp.zeros((rows, LANES), f32)) * 2
        carry = lax.fori_loop(0, i, lambda j, c: tile(j, c, qs, False), start)
        carry = tile(i, carry, qs, True)
        total = [pltpu.roll(carry[2 * a + 1], head, 1) for a in range(2)]
        local = jnp.where(inside[0], carry[1] / total[0], carry[3] / total[1])
        log_total = jnp.where(inside[0], carry[0] + jnp.log(total[0]), carry[2] + jnp.log(total[1]))
        log_rows = log_total.T
        here = pl.ds(pl.multiple_of(i * rows, rows), rows)
        lse_ref[0, 0:1, here] = log_rows[0:1, :]
        lse_ref[0, 1:2, here] = log_rows[head : head + 1, :]
        wide = q.astype(f32)
        toward_mu = wide * u_ref[0:1, :]
        toward_sig = wide * u_ref[1:2, :]
        mem = jnp.zeros((rows, LANES), f32)
        for a in range(2):
            centre_arg = jnp.sum(jnp.where(inside[a], toward_mu, 0.0), axis=1, keepdims=True)
            spread_arg = jnp.sum(jnp.where(inside[a], toward_sig, 0.0), axis=1, keepdims=True)
            centre, spread = spread_parts(centre_arg, spread_arg)
            offset = centre - centres
            density = jnp.exp(offset * offset * (-0.5 / spread)) * (width_b * lax.rsqrt(spread))
            mem = mem + mm(density.astype(bf16), mv_ref[...] * sel[a])
        loc_ref[pl.ds(at, rows), :] = local
        att_ref[pl.ds(at, rows), :] = (local + on * mem).astype(bf16)
        return 0

    lax.fori_loop(0, count, q_step, 0)


def backward_kernel(
    order, flag, q_ref, k_ref, v_ref, mv_ref, u_ref, ut_ref, g_ref, loc_ref, lse_ref,
    dqkv_ref, dmv_ref, da_ref, dq_acc, term, dmv_acc, da_acc, *, rows, count, head, scale
):
    lane = lax.broadcasted_iota(jnp.int32, (1, LANES), 1)
    inside = [lane // head == a for a in range(2)]
    sel = [jnp.where(m, 1.0, 0.0).astype(bf16) for m in inside]
    sel_scale = [jnp.where(m, scale, 0.0).astype(bf16) for m in inside]
    basis = mv_ref.shape[0]
    centres = (lax.broadcasted_iota(jnp.int32, (basis, 1), 0).astype(f32) + 0.5) / basis
    width_b = 0.75 / basis
    on = jnp.full((1, LANES), flag[0].astype(f32)).astype(bf16)
    dmv_acc[...] = jnp.zeros_like(dmv_acc)
    da_acc[...] = jnp.zeros_like(da_acc)

    def mem_step(i, _):
        at = pl.multiple_of(order[i] * rows, rows)
        here = pl.ds(pl.multiple_of(i * rows, rows), rows)
        q = q_ref[pl.ds(at, rows), :]
        g = g_ref[pl.ds(at, rows), :]
        term_t = (g.astype(f32) * loc_ref[pl.ds(at, rows), :]).T
        qt = q.astype(f32).T
        toward_mu = qt * ut_ref[:, 0:1]
        toward_sig = qt * ut_ref[:, 1:2]
        g_on = g * on
        pieces, pulls = [], []
        for a in range(2):
            lo, hi = a * head, (a + 1) * head
            term[a : a + 1, here] = jnp.sum(term_t[lo:hi, :], axis=0, keepdims=True)
            centre_arg = jnp.sum(toward_mu[lo:hi, :], axis=0, keepdims=True)
            spread_arg = jnp.sum(toward_sig[lo:hi, :], axis=0, keepdims=True)
            centre, spread = spread_parts(centre_arg, spread_arg)
            offset = centre - centres
            square = offset * offset
            density = jnp.exp(square * (-0.5 / spread)) * (width_b * lax.rsqrt(spread))
            ga = g_on * sel[a]
            pull = mm(mv_ref[...] * sel[a], g_on, NT) * density
            dmv_acc[...] += mm(density.astype(bf16), ga)
            sum0 = jnp.sum(pull, axis=0, keepdims=True)
            sum1 = jnp.sum(pull * offset, axis=0, keepdims=True)
            sum2 = jnp.sum(pull * square, axis=0, keepdims=True)
            d_centre = -sum1 / spread * centre * (1.0 - centre)
            d_spread = (sum2 / spread - sum0) * (0.5 * spread_var) / spread
            d_spread = d_spread / (1.0 + jnp.exp(-spread_arg))
            pulls += [d_centre, d_spread]
            pieces.append(ut_ref[lo:hi, 0:1] * d_centre + ut_ref[lo:hi, 1:2] * d_spread)
        dq_acc[here, :] = jnp.concatenate(pieces, axis=0).T
        stacked = jnp.concatenate(pulls + [jnp.zeros((4, rows), f32)], axis=0)
        high_part = stacked.astype(bf16)
        low_part = (stacked - high_part.astype(f32)).astype(bf16)
        da_acc[...] += mm(high_part, q) + mm(low_part, q)
        return 0

    lax.fori_loop(0, count, mem_step, 0)
    dmv_ref[...] = dmv_acc[...].astype(bf16)
    row8 = lax.broadcasted_iota(jnp.int32, (8, LANES), 0)
    da = da_acc[...]
    mu_row = jnp.where(inside[0], da[0:1, :], da[2:3, :])
    sig_row = jnp.where(inside[0], da[1:2, :], da[3:4, :])
    da_ref[...] = jnp.where(row8 == 0, mu_row, sig_row)
    behind = lax.broadcasted_iota(jnp.int32, (rows, rows), 1) >= lax.broadcasted_iota(
        jnp.int32, (rows, rows), 0
    )

    def k_step(j, _):
        at = pl.multiple_of(order[j] * rows, rows)
        k = k_ref[pl.ds(at, rows), :]
        v = v_ref[pl.ds(at, rows), :]
        ks = [k * s for s in sel_scale]
        vs = [v * s for s in sel]

        def tile(i, carry, diagonal):
            dk, dv = carry
            qat = pl.multiple_of(order[i] * rows, rows)
            here = pl.ds(pl.multiple_of(i * rows, rows), rows)
            q = q_ref[pl.ds(qat, rows), :]
            g = g_ref[pl.ds(qat, rows), :]
            dq = jnp.zeros((rows, LANES), f32)
            for a in range(2):
                s = mm(ks[a], q, NT)
                p = jnp.exp(s - lse_ref[0, a : a + 1, here])
                if diagonal:
                    p = jnp.where(behind, p, 0.0)
                dv = dv + mm(p.astype(bf16), g * sel[a])
                ds = (p * (mm(vs[a], g, NT) - term[a : a + 1, here])).astype(bf16)
                dk = dk + mm(ds, q * sel_scale[a])
                dq = dq + mm(ds, ks[a], TN)
            dq_acc[here, :] += dq
            return dk, dv

        zero = jnp.zeros((rows, LANES), f32)
        carry = tile(j, (zero, zero), True)
        dk, dv = lax.fori_loop(j + 1, count, lambda i, c: tile(i, c, False), carry)
        dqkv_ref[1, pl.ds(at, rows), :] = dk.astype(bf16)
        dqkv_ref[2, pl.ds(at, rows), :] = dv.astype(bf16)
        return 0

    lax.fori_loop(0, count, k_step, 0)

    def q_out(i, _):
        at = pl.multiple_of(order[i] * rows, rows)
        here = pl.ds(pl.multiple_of(i * rows, rows), rows)
        dqkv_ref[0, pl.ds(at, rows), :] = dq_acc[here, :].astype(bf16)
        return 0

    lax.fori_loop(0, count, q_out, 0)


def attend_segment(projected, mem_kv, u_rows, order, flag, count, head):
    total_rows = projected.shape[0]
    width = projected.shape[1] // 3
    basis = mem_kv.shape[0]
    pairs = width // LANES
    rows = total_rows // count
    scale = 1.0 / math.sqrt(head)

    def column(base):
        return pl.BlockSpec((total_rows, LANES), lambda h, *_: (0, base + h))

    tiles = total_rows * (total_rows + rows) // 2 * 2 * pairs
    return pl.pallas_call(
        partial(forward_kernel, rows=rows, count=count, head=head, scale=scale),
        grid_spec=pltpu.PrefetchScalarGridSpec(
            num_scalar_prefetch=2,
            grid=(pairs,),
            in_specs=[
                column(0),
                column(pairs),
                column(2 * pairs),
                pl.BlockSpec((basis, LANES), lambda h, *_: (0, pairs + h)),
                pl.BlockSpec((8, LANES), lambda h, *_: (0, h)),
            ],
            out_specs=[
                column(0),
                column(0),
                pl.BlockSpec((1, 2, total_rows), lambda h, *_: (h, 0, 0)),
            ],
        ),
        out_shape=[
            jax.ShapeDtypeStruct((total_rows, width), bf16),
            jax.ShapeDtypeStruct((total_rows, width), f32),
            jax.ShapeDtypeStruct((pairs, 2, total_rows), f32),
        ],
        compiler_params=pltpu.CompilerParams(vmem_limit_bytes=48 * 2**20),
        cost_estimate=pl.CostEstimate(
            flops=tiles * 4 * 256, transcendentals=tiles, bytes_accessed=12 * total_rows * width
        ),
        name="attend_forward",
    )(order, flag, projected, projected, projected, mem_kv, u_rows)


def attend_back(projected, mem_kv, u_rows, u_cols, context_grad, local, lse, order, flag, count, head):
    total_rows = projected.shape[0]
    width = projected.shape[1] // 3
    basis = mem_kv.shape[0]
    pairs = width // LANES
    rows = total_rows // count
    scale = 1.0 / math.sqrt(head)

    def column(base):
        return pl.BlockSpec((total_rows, LANES), lambda h, *_: (0, base + h))

    tiles = total_rows * (total_rows + rows) // 2 * 2 * pairs
    return pl.pallas_call(
        partial(backward_kernel, rows=rows, count=count, head=head, scale=scale),
        grid_spec=pltpu.PrefetchScalarGridSpec(
            num_scalar_prefetch=2,
            grid=(pairs,),
            in_specs=[
                column(0),
                column(pairs),
                column(2 * pairs),
                pl.BlockSpec((basis, LANES), lambda h, *_: (0, pairs + h)),
                pl.BlockSpec((8, LANES), lambda h, *_: (0, h)),
                pl.BlockSpec((LANES, 8), lambda h, *_: (h, 0)),
                column(0),
                column(0),
                pl.BlockSpec((1, 2, total_rows), lambda h, *_: (h, 0, 0)),
            ],
            out_specs=[
                pl.BlockSpec((3, total_rows, LANES), lambda h, *_: (0, 0, h)),
                pl.BlockSpec((basis, LANES), lambda h, *_: (0, h)),
                pl.BlockSpec((8, LANES), lambda h, *_: (0, h)),
            ],
            scratch_shapes=[
                pltpu.VMEM((total_rows, LANES), f32),
                pltpu.VMEM((8, total_rows), f32),
                pltpu.VMEM((basis, LANES), f32),
                pltpu.VMEM((8, LANES), f32),
            ],
        ),
        out_shape=[
            jax.ShapeDtypeStruct((3, total_rows, width), bf16),
            jax.ShapeDtypeStruct((basis, width), bf16),
            jax.ShapeDtypeStruct((8, width), f32),
        ],
        compiler_params=pltpu.CompilerParams(vmem_limit_bytes=48 * 2**20),
        cost_estimate=pl.CostEstimate(
            flops=tiles * 10 * 256, transcendentals=tiles, bytes_accessed=20 * total_rows * width
        ),
        name="attend_backward",
    )(order, flag, projected, projected, projected, mem_kv, u_rows, u_cols, context_grad, local, lse)


def density_of(queries, u_mu, u_sig, basis_count):
    highest = lax.Precision.HIGHEST
    centres = (jnp.arange(basis_count, dtype=f32) + 0.5) / basis_count
    width_b = 0.75 / basis_count
    wide = queries.astype(f32)
    centre = jax.nn.sigmoid(jnp.einsum("qhd,hd->qh", wide, u_mu, precision=highest))
    spread = spread_var * jax.nn.softplus(
        jnp.einsum("qhd,hd->qh", wide, u_sig, precision=highest)
    )
    spread = (spread + spread_floor)[..., None]
    offset = centre[..., None] - centres
    return width_b * lax.rsqrt(spread) * jnp.exp(-offset * offset / (2.0 * spread))


def spread_attend(projected, mem_kv, u_mu, u_sig, q_pos, k_pos, team, flag, heads):
    rows, width = projected.shape[0], projected.shape[1] // 3
    basis = mem_kv.shape[0]
    head = width // heads
    scale = 1.0 / math.sqrt(head)
    shape = (-1, heads, head)
    queries = projected[:, :width].reshape(shape)
    both = lax.all_gather(projected[:, width:], "blk", axis=0, tiled=True, axis_index_groups=team)
    keys, values = both[:, :width].reshape(shape), both[:, width:].reshape(shape)
    scores = jnp.einsum("qhd,khd->hqk", queries, keys, preferred_element_type=f32) * scale
    allowed = (q_pos[:, None] >= k_pos[None, :])[None]
    scores = jnp.where(allowed, scores, masked_value)
    lse = jax.nn.logsumexp(scores, axis=-1, keepdims=True)
    probs = jnp.where(allowed, jnp.exp(scores - lse), 0.0)
    local = jnp.einsum("hqk,khd->qhd", probs.astype(bf16), values, preferred_element_type=f32)
    mem_values = mem_kv[:, width:].reshape(shape)
    density = density_of(queries, u_mu, u_sig, basis).astype(bf16)
    mem = jnp.einsum("qhn,nhd->qhd", density, mem_values, preferred_element_type=f32)
    attended = (local + flag.astype(f32) * mem).astype(bf16).reshape(rows, width)
    return attended, (queries, keys, values, probs, local, density, mem_values)


def spread_back(kept, context_grad, u_mu, u_sig, team, flag):
    queries, keys, values, probs, local, density, mem_values = kept
    rows, heads, head = queries.shape
    basis = mem_values.shape[0]
    scale = 1.0 / math.sqrt(head)
    g = context_grad.reshape(queries.shape)
    term = jnp.sum(g.astype(f32) * local, axis=-1)
    dv = jnp.einsum("hqk,qhd->khd", probs.astype(bf16), g, preferred_element_type=f32)
    dp = jnp.einsum("qhd,khd->hqk", g, values, preferred_element_type=f32)
    ds = (probs * (dp - term.T[..., None])).astype(bf16)
    dq = jnp.einsum("hqk,khd->qhd", ds, keys, preferred_element_type=f32) * scale
    dk = jnp.einsum("hqk,qhd->khd", ds, queries, preferred_element_type=f32) * scale
    both = jnp.stack([dk.reshape(-1, heads * head), dv.reshape(-1, heads * head)], 1).astype(bf16)
    both = lax.psum_scatter(both, "blk", scatter_dimension=0, tiled=True, axis_index_groups=team)
    g_on = g * flag.astype(bf16)
    pull = jnp.einsum("qhd,nhd->qhn", g_on, mem_values, preferred_element_type=f32)
    dmv = jnp.einsum("qhn,qhd->nhd", density, g_on, preferred_element_type=f32)
    dq_mem, d_mu, d_sig = jax.vjp(
        lambda q, m, s: density_of(q, m, s, basis), queries.astype(f32), u_mu, u_sig
    )[1](pull)
    dqkv = jnp.stack([(dq + dq_mem).reshape(rows, -1).astype(bf16), both[:, 0], both[:, 1]])
    return dqkv, dmv.reshape(basis, -1), d_mu.reshape(1, -1), d_sig.reshape(1, -1)


def per_device(
    tokens,
    memory,
    present,
    block_pos,
    ln1_gain,
    ln1_bias,
    w_qkv,
    w_out,
    ln2_gain,
    ln2_bias,
    w_fc,
    w_proj,
    w_mu,
    w_sig,
    grad_out,
    grad_memory,
):
    members, seg_rows, model_width = tokens.shape
    blocks = lax.axis_size("blk")
    teams = blocks // members
    heads, basis = w_mu.shape
    head = model_width // heads
    total_rows = members * seg_rows
    seg_len = seg_rows * blocks
    scale = 1.0 / math.sqrt(head)
    rank = lax.axis_index("blk")
    member, team_rank = rank % members, rank // members
    team = [[s + members * j for j in range(teams)] for s in range(members)]

    token_slots = collect_blocks(tokens, members)
    token_slots, grad_out = lax.optimization_barrier((token_slots, grad_out))
    grad_slots = collect_blocks(grad_out, members)
    inputs_low = jnp.concatenate(token_slots, axis=0)
    mem = pick(memory, member)
    mem_cot = pick(grad_memory, member)
    flag = lax.dynamic_slice_in_dim(present, member, 1, 0)
    on = flag[0].astype(f32)
    seg_order = pick(block_pos, member)
    back = (member - jnp.arange(members, dtype=jnp.int32)) % members
    slot_pos = seg_order[team_rank * members + back]

    ridge_table, carry_table = memory_tables(basis, seg_len)
    ridge_parts = [
        jnp.asarray(part.reshape(basis, blocks, seg_rows).transpose(1, 0, 2))[slot_pos]
        for part in split_low(ridge_table)
    ]
    carry_parts = [jnp.asarray(part) for part in split_low(carry_table)]

    inputs = inputs_low.astype(f32)
    normed_one, unit_one, inverse_one = norm_rows(inputs, ln1_gain, ln1_bias)
    normed_low = normed_one.astype(bf16)
    projected = mm(normed_low, w_qkv).astype(bf16)
    mem_kv = mm(mem, w_qkv[:, model_width:]).astype(bf16)
    mem_keys = mem_kv[:, :model_width].astype(f32)
    wide_mu = jnp.repeat(w_mu.T, head, axis=1)
    wide_sig = jnp.repeat(w_sig.T, head, axis=1)
    u_mu = scale * jnp.sum(mem_keys * wide_mu, axis=0)
    u_sig = scale * jnp.sum(mem_keys * wide_sig, axis=0)

    if teams == 1:
        order = jnp.argmax(
            slot_pos[None, :] == jnp.arange(members, dtype=jnp.int32)[:, None], axis=1
        ).astype(jnp.int32)
        u_rows = jnp.zeros((8, model_width), f32).at[0].set(u_mu).at[1].set(u_sig)
        u_cols = jnp.zeros((model_width, 8), f32).at[:, 0].set(u_mu).at[:, 1].set(u_sig)
        attended, local, lse = attend_segment(
            projected, mem_kv, u_rows, order, flag, members, head
        )
    else:
        row_ids = jnp.arange(seg_rows, dtype=jnp.int32)
        q_pos = (slot_pos[:, None] * seg_rows + row_ids[None, :]).reshape(-1)
        key_order = seg_order.reshape(teams, members)[:, back]
        k_pos = (key_order[:, :, None] * seg_rows + row_ids).reshape(-1)
        mu_heads, sig_heads = u_mu.reshape(heads, head), u_sig.reshape(heads, head)
        attended, kept = spread_attend(
            projected, mem_kv, mu_heads, sig_heads, q_pos, k_pos, team, flag, heads
        )

    middle = inputs + mm(attended, w_out)
    normed_two, unit_two, inverse_two = norm_rows(middle, ln2_gain, ln2_bias)
    second = normed_two.astype(bf16)
    hidden_pre = mm(second, w_fc)
    hidden = jax.nn.gelu(hidden_pre, approximate=True).astype(bf16)
    result_rows = (middle + mm(hidden, w_proj)).astype(bf16)
    result = return_blocks(
        [result_rows[d * seg_rows : (d + 1) * seg_rows] for d in range(members)], members
    )

    rows_of = normed_low.reshape(members, seg_rows, model_width)
    gathered = sum(
        jnp.einsum("pnr,prd->nd", part, rows_of, preferred_element_type=f32)
        for part in ridge_parts
    )
    if teams > 1:
        gathered = lax.psum(gathered, "blk", axis_index_groups=team)
    new_memory = (on * sum(mm(part, mem) for part in carry_parts) + gathered).astype(bf16)

    out_rows = jnp.concatenate(grad_slots, axis=0)
    w_proj_grad = sum_weight(mm(hidden, out_rows, TN))
    hidden_grad = mm(out_rows, w_proj, NT)
    gelu_pull = jax.vjp(partial(jax.nn.gelu, approximate=True), hidden_pre)[1]
    pre_grad = gelu_pull(hidden_grad)[0].astype(bf16)
    w_fc_grad = sum_weight(mm(second, pre_grad, TN))
    back_two, ln2_gain_grad, ln2_bias_grad = norm_back(
        mm(pre_grad, w_fc, NT), unit_two, inverse_two, ln2_gain
    )
    middle_grad = out_rows.astype(f32) + back_two
    branch_grad = middle_grad.astype(bf16)
    w_out_grad = sum_weight(mm(attended, branch_grad, TN))
    context_grad = mm(branch_grad, w_out, NT).astype(bf16)

    if teams == 1:
        dqkv, mem_values_grad, pulls = attend_back(
            projected, mem_kv, u_rows, u_cols, context_grad, local, lse, order, flag, members, head
        )
        mu_part, sig_part = pulls[0:1], pulls[1:2]
        mu_sum, sig_sum = scale * mu_part, scale * sig_part
    else:
        dqkv, mem_values_grad, mu_part, sig_part = spread_back(
            kept, context_grad, mu_heads, sig_heads, team, flag
        )
        mu_part, sig_part = scale * mu_part, scale * sig_part
        mem_values_grad, mu_sum, sig_sum = lax.psum(
            (mem_values_grad, mu_part, sig_part), "blk", axis_index_groups=team
        )
        mem_values_grad = mem_values_grad.astype(bf16)
    if teams == 1:
        mu_part, sig_part = mu_sum, sig_sum
    mem_keys_grad = (wide_mu * mu_sum + wide_sig * sig_sum).astype(bf16)
    w_mu_grad = jnp.sum((mem_keys * mu_part).reshape(basis, heads, head), axis=2).T
    w_sig_grad = jnp.sum((mem_keys * sig_part).reshape(basis, heads, head), axis=2).T

    first_team = (team_rank == 0).astype(bf16)
    mem_once = mem * first_team
    w_qkv_parts = [mm(normed_low, dqkv[0], TN)]
    w_qkv_parts.append(mm(normed_low, dqkv[1], TN) + mm(mem_once, mem_keys_grad, TN))
    w_qkv_parts.append(mm(normed_low, dqkv[2], TN) + mm(mem_once, mem_values_grad, TN))
    w_qkv_grad = sum_weight(jnp.concatenate(w_qkv_parts, axis=1))

    memory_grad = (
        on
        * (
            mm(mem_keys_grad, w_qkv[:, model_width : 2 * model_width], NT)
            + mm(mem_values_grad, w_qkv[:, 2 * model_width :], NT)
            + sum(mm(part, mem_cot, TN) for part in carry_parts)
        )
    ).astype(bf16)
    normed_one_grad = sum(
        mm(dqkv[c], w_qkv[:, c * model_width : (c + 1) * model_width], NT) for c in range(3)
    )
    normed_one_grad = normed_one_grad + sum(
        jnp.einsum("pnr,nd->prd", part, mem_cot, preferred_element_type=f32)
        for part in ridge_parts
    ).reshape(total_rows, model_width)
    back_one, ln1_gain_grad, ln1_bias_grad = norm_back(
        normed_one_grad, unit_one, inverse_one, ln1_gain
    )
    token_grad = (middle_grad + back_one).astype(bf16)
    grad_tokens = return_blocks(
        [token_grad[d * seg_rows : (d + 1) * seg_rows] for d in range(members)], members
    )
    new_memory = share_segments(new_memory, members)
    memory_grad = share_segments(memory_grad, members)
    early = lax.psum((ln2_gain_grad, ln2_bias_grad, w_mu_grad, w_sig_grad), ("seg", "blk"))
    ln2_gain_grad, ln2_bias_grad, w_mu_grad, w_sig_grad = early
    ln1_gain_grad, ln1_bias_grad = lax.psum((ln1_gain_grad, ln1_bias_grad), ("seg", "blk"))
    return (
        result,
        new_memory,
        grad_tokens,
        memory_grad,
        ln1_gain_grad,
        ln1_bias_grad,
        w_qkv_grad,
        w_out_grad,
        ln2_gain_grad,
        ln2_bias_grad,
        w_fc_grad,
        w_proj_grad,
        w_mu_grad,
        w_sig_grad,
    )


def solution(mesh):
    split = P("seg", "blk", None)
    whole_seg = P("seg", None, None)
    return jax.shard_map(
        per_device,
        mesh=mesh,
        in_specs=(split, whole_seg, P("seg"), P("seg", None)) + (P(),) * 10 + (split, whole_seg),
        out_specs=(split, whole_seg, split, whole_seg) + (P(),) * 10,
        check_vma=False,
    )
```

```python
from functools import partial
import math

import jax
import jax.numpy as jnp
import ml_dtypes
import numpy as np
from jax import lax
from jax.experimental import pallas as pl
from jax.experimental.pallas import tpu as pltpu
from jax.sharding import PartitionSpec as P

eps_norm = 1e-05
ridge_weight = 1.0
contract = 0.5
spread_var = 0.05
spread_floor = 0.002
masked_value = -1e30
LANES = 128
f32 = jnp.float32
bf16 = jnp.bfloat16

NN = (((1,), (0,)), ((), ()))
NT = (((1,), (1,)), ((), ()))
TN = (((0,), (0,)), ((), ()))


def mm(a, b, dims=NN):
    return lax.dot_general(a, b, dims, preferred_element_type=f32)


def basis_table(points, basis_count):
    centres = (np.arange(basis_count, dtype=np.float64) + 0.5) / basis_count
    width_b = 0.75 / basis_count
    offset = points[..., None] - centres
    return np.exp(-offset * offset / (2.0 * width_b * width_b))


def split_low(table):
    high_part = table.astype(ml_dtypes.bfloat16)
    low_part = (table - high_part.astype(np.float64)).astype(ml_dtypes.bfloat16)
    return high_part, low_part


def memory_tables(basis_count, seg_len):
    samples = (np.arange(basis_count, dtype=np.float64) + 0.5) / basis_count
    squeezed = basis_table(contract * samples, basis_count)
    stretched = basis_table(samples, basis_count)
    carry_map = squeezed.T @ stretched
    times = contract + (1.0 - contract) * (np.arange(seg_len, dtype=np.float64) + 0.5) / seg_len
    all_times = basis_table(times, basis_count)
    gram = squeezed.T @ squeezed + all_times.T @ all_times + ridge_weight * np.eye(basis_count)
    return np.linalg.solve(gram, all_times.T), np.linalg.solve(gram, carry_map)


def digit_route(size, stride, radix, distance):
    route = []
    for i in range(size):
        digit = (i // stride) % radix
        route.append((i, i + ((digit + distance) % radix - digit) * stride))
    return route


def pick(stack, index):
    return lax.dynamic_index_in_dim(stack, index, 0, keepdims=False)


def put(stack, block, index):
    return lax.dynamic_update_index_in_dim(stack, block, index, 0)


class ScatterStep:
    def __init__(self, parts, axis, stride, radix):
        size = lax.axis_size(axis)
        digit = (lax.axis_index(axis) // stride) % radix
        self.own = pick(parts, digit) if radix > 1 else parts[0]
        self.got = [
            lax.ppermute(
                pick(parts, (digit + distance) % radix), axis, digit_route(size, stride, radix, distance)
            )
            for distance in range(1, radix)
        ]

    def complete(self):
        total = self.own.astype(f32)
        for part in self.got:
            total = total + part.astype(f32)
        return total.astype(bf16)


class GatherStep:
    def __init__(self, block, axis, stride, radix):
        size = lax.axis_size(axis)
        self.digit = (lax.axis_index(axis) // stride) % radix
        self.radix = radix
        self.own = block
        self.got = [
            lax.ppermute(block, axis, digit_route(size, stride, radix, distance))
            for distance in range(1, radix)
        ]

    def complete(self):
        stack = jnp.zeros((self.radix,) + self.own.shape, self.own.dtype)
        stack = put(stack, self.own, self.digit)
        for distance, part in enumerate(self.got, 1):
            stack = put(stack, part, (self.digit - distance) % self.radix)
        return stack


def sum_step(block, axis, stride, radix):
    size = lax.axis_size(axis)
    total = block.astype(f32)
    for distance in range(1, radix):
        total = total + lax.ppermute(block, axis, digit_route(size, stride, radix, distance)).astype(f32)
    return total.astype(block.dtype)


def gather_step(block, axis, stride, radix):
    return GatherStep(block, axis, stride, radix).complete()


def near(size):
    return 2 if size % 2 == 0 else 1


class WeightSum:
    def __init__(self, block, order):
        blk, seg = lax.axis_size("blk"), lax.axis_size("seg")
        core, side = near(blk), near(seg)
        digits = {
            "core": ("blk", 1, core),
            "y": ("blk", core, blk // core),
            "x": ("seg", 1, side),
            "z": ("seg", side, seg // side),
        }
        self.block = block
        self.steps = [(True,) + digits[name] for name in order]
        self.steps += [(False,) + digits[name] for name in reversed(order)]

        self.now = None

    def begin(self):
        if not self.steps:
            return []
        inward, axis, stride, radix = self.steps.pop(0)
        rows, columns = self.block.shape
        if inward:
            self.now = ScatterStep(self.block.reshape(radix, rows // radix, columns), axis, stride, radix)
            self.rows = rows // radix
        else:
            self.now = GatherStep(self.block, axis, stride, radix)
            self.rows = rows * radix
        return [self.now.own]

    def complete(self, own):
        if own:
            self.now.own = own[0]
            self.block = self.now.complete().reshape(self.rows, self.block.shape[1])

    def finish(self):
        while self.steps:
            self.complete(self.begin())
        return self.block


def sum_all(block):
    blk, seg = lax.axis_size("blk"), lax.axis_size("seg")
    core, side = near(blk), near(seg)
    block = sum_step(block, "blk", 1, core)
    block = sum_step(block, "seg", 1, side)
    block = sum_step(block, "blk", core, blk // core)
    return sum_step(block, "seg", side, seg // side)


def collect_blocks(stack, members):
    size = lax.axis_size("blk")
    member = lax.axis_index("blk") % members
    slots = [pick(stack, member)]
    for distance in range(1, members):
        sent = pick(stack, (member + distance) % members)
        slots.append(lax.ppermute(sent, "blk", digit_route(size, 1, members, distance)))
    return slots


class ReturnBlocks:
    def __init__(self, rows, members):
        size = lax.axis_size("blk")
        count = rows.shape[0] // members
        slots = [rows[d * count : (d + 1) * count] for d in range(members)]
        self.member = lax.axis_index("blk") % members
        self.members = members
        self.own = slots[0]
        self.got = [
            lax.ppermute(slots[distance], "blk", digit_route(size, 1, members, members - distance))
            for distance in range(1, members)
        ]

    def begin(self):
        return [self.own]

    def complete(self, own):
        self.own = own[0]

    def finish(self):
        stack = jnp.zeros((self.members,) + self.own.shape, self.own.dtype)
        stack = put(stack, self.own, self.member)
        for distance, part in enumerate(self.got, 1):
            stack = put(stack, part, (self.member + distance) % self.members)
        return stack


def beside(moves, call):
    begun = [move.begin() for move in moves]
    flat = [part for parts in begun for part in parts]
    outputs, flat = call(flat)
    for move, parts in zip(moves, begun):
        move.complete(flat[: len(parts)])
        flat = flat[len(parts) :]
    return outputs


def share_segments(block, members):
    size = members
    if members % 2 == 0:
        stack = gather_step(block, "blk", 2, members // 2)
        stack = gather_step(stack, "blk", 1, 2)
        return jnp.swapaxes(stack, 0, 1).reshape((size,) + block.shape)
    return gather_step(block, "blk", 1, members)


def spread_parts(centre_arg, spread_arg):
    centre = 1.0 / (1.0 + jnp.exp(-centre_arg))
    tail = jnp.exp(-jnp.abs(spread_arg))
    spread = spread_var * (jnp.maximum(spread_arg, 0.0) + jnp.log(1.0 + tail)) + spread_floor
    return centre, spread


def forward_kernel(
    order, flag, q_ref, k_ref, v_ref, mv_ref, ut_ref, att_ref, loc_ref, lse_ref, vt, *, rows, count, head, scale
):
    lane = lax.broadcasted_iota(jnp.int32, (1, LANES), 1)
    sel_scale = [jnp.where(lane // head == a, scale, 0.0).astype(bf16) for a in range(2)]
    basis = mv_ref.shape[0]
    centres = (lax.broadcasted_iota(jnp.int32, (basis, 1), 0).astype(f32) + 0.5) / basis
    width_b = 0.75 / basis
    on = flag[0].astype(f32)
    half = rows // 2
    mv_t = mv_ref[...].astype(f32).T.astype(bf16)
    ones = jnp.ones((head, rows), bf16)

    def turn(j, _):
        here = pl.ds(pl.multiple_of(j * rows, rows), rows)
        v_t = v_ref[here, :].astype(f32).T.astype(bf16)
        vt[0, :, here] = jnp.concatenate([v_t[:head, :], ones], axis=0)
        vt[1, :, here] = jnp.concatenate([ones, v_t[head:, :]], axis=0)
        return 0

    lax.fori_loop(0, count, turn, 0)

    def absorb(carry, qs, k, v_t, masked):
        out = []
        for a in range(2):
            top, acc = carry[2 * a], carry[2 * a + 1]
            s = mm(k, qs[a], NT)
            if masked:
                key_id = lax.broadcasted_iota(jnp.int32, s.shape, 0)
                s = jnp.where(lax.broadcasted_iota(jnp.int32, s.shape, 1) >= key_id, s, masked_value)
            new_top = jnp.maximum(top, jnp.max(s, axis=0, keepdims=True))
            p = jnp.exp(s - new_top)
            acc = acc * jnp.exp(top - new_top) + mm(v_t[a], p.astype(bf16))
            out += [new_top, acc]
        return tuple(out)

    def q_step(i, _):
        at = pl.multiple_of(order[i] * rows, rows)
        q = q_ref[pl.ds(at, rows), :]
        qs = [q * s for s in sel_scale]
        start = (jnp.full((1, rows), masked_value, f32), jnp.zeros((LANES, rows), f32)) * 2

        def tile(j, carry):
            kat = pl.multiple_of(order[j] * rows, rows)
            v_t = [vt[a, :, pl.ds(kat, rows)] for a in range(2)]
            return absorb(carry, qs, k_ref[pl.ds(kat, rows), :], v_t, False)

        carry = lax.fori_loop(0, i, tile, start)
        k = k_ref[pl.ds(at, half), :]
        v_t = [vt[a, :, pl.ds(at, half)] for a in range(2)]
        carry = absorb(carry, qs, k, v_t, True)
        at_late = pl.multiple_of(at + half, half)
        k = k_ref[pl.ds(at_late, half), :]
        v_t = [vt[a, :, pl.ds(at_late, half)] for a in range(2)]
        late = absorb(tuple(c[:, half:] for c in carry), [x[half:] for x in qs], k, v_t, True)
        carry = [jnp.concatenate([c[:, :half], d], axis=1) for c, d in zip(carry, late)]
        here = pl.ds(pl.multiple_of(i * rows, rows), rows)
        total = [carry[1][head : head + 1, :], carry[3][0:1, :]]
        local = jnp.concatenate([carry[1][:head] / total[0], carry[3][head:] / total[1]], axis=0)
        for a in range(2):
            lse_ref[0, a : a + 1, here] = carry[2 * a] + jnp.log(total[a])
        q_t = q.astype(f32).T
        toward_mu = q_t * ut_ref[:, 0:1]
        toward_sig = q_t * ut_ref[:, 1:2]
        mem = []
        for a in range(2):
            lo, hi = a * head, (a + 1) * head
            centre_arg = jnp.sum(toward_mu[lo:hi], axis=0, keepdims=True)
            spread_arg = jnp.sum(toward_sig[lo:hi], axis=0, keepdims=True)
            centre, spread = spread_parts(centre_arg, spread_arg)
            offset = centre - centres
            density = jnp.exp(offset * offset * (-0.5 / spread)) * (width_b * lax.rsqrt(spread))
            mem.append(mm(mv_t[lo:hi], density.astype(bf16)))
        loc_ref[pl.ds(at, rows), :] = local.T
        att_ref[pl.ds(at, rows), :] = (local + on * jnp.concatenate(mem, axis=0)).T.astype(bf16)
        return 0

    lax.fori_loop(0, count, q_step, 0)


def backward_kernel(
    order, flag, q_ref, k_ref, v_ref, mv_ref, ut_ref, g_ref, loc_ref, lse_ref, *refs,
    rows, count, head, scale, skip
):
    dqkv_ref, dmv_ref, da_ref = refs[skip : skip + 3]
    dq_acc, kt, term, dmv_acc, da_acc = refs[-5:]
    lane = lax.broadcasted_iota(jnp.int32, (1, LANES), 1)
    inside = [lane // head == a for a in range(2)]
    sel = [jnp.where(m, 1.0, 0.0).astype(bf16) for m in inside]
    sel_scale = [jnp.where(m, scale, 0.0).astype(bf16) for m in inside]
    basis = mv_ref.shape[0]
    centres = (lax.broadcasted_iota(jnp.int32, (basis, 1), 0).astype(f32) + 0.5) / basis
    width_b = 0.75 / basis
    on = jnp.full((1, LANES), flag[0].astype(f32)).astype(bf16)
    half = rows // 2
    dmv_acc[...] = jnp.zeros_like(dmv_acc)
    da_acc[...] = jnp.zeros_like(da_acc)

    def mem_step(i, _):
        at = pl.multiple_of(order[i] * rows, rows)
        here = pl.ds(pl.multiple_of(i * rows, rows), rows)
        q = q_ref[pl.ds(at, rows), :]
        g = g_ref[pl.ds(at, rows), :]
        kt[:, pl.ds(at, rows)] = (k_ref[pl.ds(at, rows), :].astype(f32) * scale).T.astype(bf16)
        term_t = (g.astype(f32) * loc_ref[pl.ds(at, rows), :]).T
        qt = q.astype(f32).T
        toward_mu = qt * ut_ref[:, 0:1]
        toward_sig = qt * ut_ref[:, 1:2]
        g_on = g * on
        pulls = []
        for a in range(2):
            lo, hi = a * head, (a + 1) * head
            term[a : a + 1, here] = jnp.sum(term_t[lo:hi, :], axis=0, keepdims=True)
            centre_arg = jnp.sum(toward_mu[lo:hi, :], axis=0, keepdims=True)
            spread_arg = jnp.sum(toward_sig[lo:hi, :], axis=0, keepdims=True)
            centre, spread = spread_parts(centre_arg, spread_arg)
            offset = centre - centres
            square = offset * offset
            density = jnp.exp(square * (-0.5 / spread)) * (width_b * lax.rsqrt(spread))
            ga = g_on * sel[a]
            pull = mm(mv_ref[...] * sel[a], g_on, NT) * density
            dmv_acc[...] += mm(density.astype(bf16), ga)
            sum0 = jnp.sum(pull, axis=0, keepdims=True)
            sum1 = jnp.sum(pull * offset, axis=0, keepdims=True)
            sum2 = jnp.sum(pull * square, axis=0, keepdims=True)
            d_centre = -sum1 / spread * centre * (1.0 - centre)
            d_spread = (sum2 / spread - sum0) * (0.5 * spread_var) / spread
            d_spread = d_spread / (1.0 + jnp.exp(-spread_arg))
            pulls += [d_centre, d_spread]
            dq_acc[lo:hi, here] = ut_ref[lo:hi, 0:1] * d_centre + ut_ref[lo:hi, 1:2] * d_spread
        stacked = jnp.concatenate(pulls + [jnp.zeros((4, rows), f32)], axis=0)
        high_part = stacked.astype(bf16)
        low_part = (stacked - high_part.astype(f32)).astype(bf16)
        da_acc[...] += mm(high_part, q) + mm(low_part, q)
        return 0

    lax.fori_loop(0, count, mem_step, 0)
    dmv_ref[...] = dmv_acc[...].astype(bf16)
    row8 = lax.broadcasted_iota(jnp.int32, (8, LANES), 0)
    da = da_acc[...]
    mu_row = jnp.where(inside[0], da[0:1, :], da[2:3, :])
    sig_row = jnp.where(inside[0], da[1:2, :], da[3:4, :])
    da_ref[...] = jnp.where(row8 == 0, mu_row, sig_row)

    def pull_tile(dk, dv, ks, vs, kat, qat, here, size_k, size_q, masked):
        q = q_ref[pl.ds(qat, size_q), :]
        g = g_ref[pl.ds(qat, size_q), :]
        for a in range(2):
            lo, hi = a * head, (a + 1) * head
            s = mm(ks[a], q, NT)
            p = jnp.exp(s - lse_ref[0, a : a + 1, here])
            if masked:
                key_id = lax.broadcasted_iota(jnp.int32, s.shape, 0)
                p = jnp.where(lax.broadcasted_iota(jnp.int32, s.shape, 1) >= key_id, p, 0.0)
            ds = (p * (mm(vs[a], g, NT) - term[a : a + 1, here])).astype(bf16)
            dv = dv + mm(p.astype(bf16), g * sel[a])
            dk = dk + mm(ds, q * sel_scale[a])
            dq_acc[lo:hi, here] += mm(kt[lo:hi, pl.ds(kat, size_k)], ds)
        return dk, dv

    def k_step(j, _):
        at = pl.multiple_of(order[j] * rows, rows)
        k = k_ref[pl.ds(at, rows), :]
        v = v_ref[pl.ds(at, rows), :]
        ks = [k * s for s in sel_scale]
        vs = [v * s for s in sel]
        zero = jnp.zeros((half, LANES), f32)
        here = pl.multiple_of(j * rows, rows)
        early = pull_tile(
            zero, zero, [x[:half] for x in ks], [x[:half] for x in vs], at, at,
            pl.ds(here, rows), half, rows, True
        )
        at_late = pl.multiple_of(at + half, half)
        late = pull_tile(
            zero, zero, [x[half:] for x in ks], [x[half:] for x in vs], at_late, at_late,
            pl.ds(pl.multiple_of(here + half, half), half), half, half, True
        )
        carry = tuple(jnp.concatenate([x, y], axis=0) for x, y in zip(early, late))

        def tile(i, carry):
            qat = pl.multiple_of(order[i] * rows, rows)
            there = pl.ds(pl.multiple_of(i * rows, rows), rows)
            return pull_tile(carry[0], carry[1], ks, vs, at, qat, there, rows, rows, False)

        dk, dv = lax.fori_loop(j + 1, count, tile, carry)
        dqkv_ref[1, pl.ds(at, rows), :] = dk.astype(bf16)
        dqkv_ref[2, pl.ds(at, rows), :] = dv.astype(bf16)
        return 0

    lax.fori_loop(0, count, k_step, 0)

    def q_out(i, _):
        at = pl.multiple_of(order[i] * rows, rows)
        here = pl.ds(pl.multiple_of(i * rows, rows), rows)
        dqkv_ref[0, pl.ds(at, rows), :] = dq_acc[:, here].T.astype(bf16)
        return 0

    lax.fori_loop(0, count, q_out, 0)


def attend_segment(projected, mem_kv, u_cols, order, flag, count, head):
    total_rows = projected.shape[0]
    width = projected.shape[1] // 3
    basis = mem_kv.shape[0]
    pairs = width // LANES
    rows = total_rows // count
    scale = 1.0 / math.sqrt(head)

    def column(base):
        return pl.BlockSpec((total_rows, LANES), lambda h, *_: (0, base + h))

    tiles = total_rows * (total_rows + rows) // 2 * 2 * pairs
    return pl.pallas_call(
        partial(forward_kernel, rows=rows, count=count, head=head, scale=scale),
        grid_spec=pltpu.PrefetchScalarGridSpec(
            num_scalar_prefetch=2,
            grid=(pairs,),
            in_specs=[
                column(0),
                column(pairs),
                column(2 * pairs),
                pl.BlockSpec((basis, LANES), lambda h, *_: (0, pairs + h)),
                pl.BlockSpec((LANES, 8), lambda h, *_: (h, 0)),
            ],
            out_specs=[
                column(0),
                column(0),
                pl.BlockSpec((1, 2, total_rows), lambda h, *_: (h, 0, 0)),
            ],
            scratch_shapes=[pltpu.VMEM((2, LANES, total_rows), bf16)],
        ),
        out_shape=[
            jax.ShapeDtypeStruct((total_rows, width), bf16),
            jax.ShapeDtypeStruct((total_rows, width), f32),
            jax.ShapeDtypeStruct((pairs, 2, total_rows), f32),
        ],
        compiler_params=pltpu.CompilerParams(vmem_limit_bytes=48 * 2**20),
        cost_estimate=pl.CostEstimate(
            flops=tiles * 4 * 256, transcendentals=tiles, bytes_accessed=12 * total_rows * width
        ),
        name="attend_forward",
    )(order, flag, projected, projected, projected, mem_kv, u_cols)


def attend_back(pair, kept, projected, mem_kv, u_cols, context_grad, local, lse, order, flag, count, head, parts):
    total_rows = projected.shape[0]
    width = projected.shape[1] // 3
    basis = mem_kv.shape[0]
    pairs = width // LANES
    rows = total_rows // count
    scale = 1.0 / math.sqrt(head)

    def column(base):
        return pl.BlockSpec((total_rows, LANES), lambda h, *_: (0, base + pair))

    tiles = total_rows * (total_rows + rows) // 2 * 2
    kept = list(kept) if kept is not None else []
    extra = kept + list(parts)
    outputs = pl.pallas_call(
        partial(backward_kernel, rows=rows, count=count, head=head, scale=scale, skip=len(extra)),
        grid_spec=pltpu.PrefetchScalarGridSpec(
            num_scalar_prefetch=2,
            grid=(1,),
            in_specs=[
                column(0),
                column(pairs),
                column(2 * pairs),
                pl.BlockSpec((basis, LANES), lambda h, *_: (0, pairs + pair)),
                pl.BlockSpec((LANES, 8), lambda h, *_: (pair, 0)),
                column(0),
                column(0),
                pl.BlockSpec((1, 2, total_rows), lambda h, *_: (pair, 0, 0)),
            ]
            + [pl.BlockSpec(memory_space=pl.ANY)] * len(extra),
            out_specs=[
                pl.BlockSpec((3, total_rows, LANES), lambda h, *_: (0, 0, pair)),
                pl.BlockSpec((basis, LANES), lambda h, *_: (0, pair)),
                pl.BlockSpec((8, LANES), lambda h, *_: (0, pair)),
            ]
            + [pl.BlockSpec(memory_space=pl.ANY)] * len(parts),
            scratch_shapes=[
                pltpu.VMEM((LANES, total_rows), f32),
                pltpu.VMEM((LANES, total_rows), bf16),
                pltpu.VMEM((8, total_rows), f32),
                pltpu.VMEM((basis, LANES), f32),
                pltpu.VMEM((8, LANES), f32),
            ],
        ),
        out_shape=[
            jax.ShapeDtypeStruct((3, total_rows, width), bf16),
            jax.ShapeDtypeStruct((basis, width), bf16),
            jax.ShapeDtypeStruct((8, width), f32),
        ]
        + [jax.ShapeDtypeStruct(part.shape, part.dtype) for part in parts],
        input_output_aliases={10 + c: c + 3 - len(kept) for c in range(len(extra))},
        compiler_params=pltpu.CompilerParams(vmem_limit_bytes=48 * 2**20),
        cost_estimate=pl.CostEstimate(
            flops=tiles * 10 * 256, transcendentals=tiles, bytes_accessed=20 * total_rows * LANES
        ),
        name=f"attend_backward_{pair}",
    )(
        order, flag, projected, projected, projected, mem_kv, u_cols, context_grad, local, lse, *extra
    )
    return outputs[:3], outputs[3:]


def row_stats(values):
    centred = values - jnp.mean(values, axis=-1, keepdims=True)
    inverse = lax.rsqrt(jnp.mean(centred * centred, axis=-1, keepdims=True) + eps_norm)
    return centred * inverse, inverse


def pull_norm(upstream, unit_rows, inverse, gain_vec):
    scaled = upstream * gain_vec
    return inverse * (
        scaled
        - jnp.mean(scaled, axis=-1, keepdims=True)
        - unit_rows * jnp.mean(scaled * unit_rows, axis=-1, keepdims=True)
    )


def front_kernel(pos, x_ref, gain, bias, w_ref, high_ref, low_ref, normed_ref, proj_ref, sum_ref):
    unit, _ = row_stats(x_ref[...].astype(f32))
    normed = (unit * gain[...] + bias[...]).astype(bf16)
    normed_ref[...] = normed
    width = normed.shape[1]
    for c in range(3):
        cols = slice(c * width, (c + 1) * width)
        proj_ref[:, cols] = mm(normed, w_ref[:, cols]).astype(bf16)

    @pl.when(pl.program_id(0) == 0)
    def _():
        sum_ref[...] = jnp.zeros_like(sum_ref)

    sum_ref[...] += mm(high_ref[...], normed) + mm(low_ref[...], normed)


def front(inputs, gain, bias, w_qkv, tables, slot_pos, rows):
    total_rows, width = inputs.shape
    basis = tables[0].shape[0]
    count = total_rows // rows
    whole = lambda shape: pl.BlockSpec(shape, lambda i, pos: (0, 0), pipeline_mode=pl.Buffered(1))
    ridge = pl.BlockSpec((basis, rows), lambda i, pos: (0, pos[i]))
    return pl.pallas_call(
        front_kernel,
        grid_spec=pltpu.PrefetchScalarGridSpec(
            num_scalar_prefetch=1,
            grid=(count,),
            in_specs=[
                pl.BlockSpec((rows, width), lambda i, pos: (i, 0)),
                whole((1, width)),
                whole((1, width)),
                whole(w_qkv.shape),
                ridge,
                ridge,
            ],
            out_specs=[
                pl.BlockSpec((rows, width), lambda i, pos: (i, 0)),
                pl.BlockSpec((rows, 3 * width), lambda i, pos: (i, 0)),
                pl.BlockSpec((basis, width), lambda i, pos: (0, 0)),
            ],
        ),
        out_shape=[
            jax.ShapeDtypeStruct((total_rows, width), bf16),
            jax.ShapeDtypeStruct((total_rows, 3 * width), bf16),
            jax.ShapeDtypeStruct((basis, width), f32),
        ],
        compiler_params=pltpu.CompilerParams(vmem_limit_bytes=40 * 2**20),
        cost_estimate=pl.CostEstimate(
            flops=2 * total_rows * width * (3 * width + 2 * basis),
            transcendentals=0,
            bytes_accessed=10 * total_rows * width + 2 * w_qkv.size,
        ),
        name="front",
    )(slot_pos, inputs, gain[None], bias[None], w_qkv, *tables)


gelu_in = math.sqrt(2.0 / math.pi)
gelu_cube = 0.044715


def middle_kernel(
    x_ref, att_ref, go_ref, gain, bias, w_out, w_fc, w_proj,
    res_ref, mid_ref, ctx_ref, d_out, d_fc, d_proj, d_vec, out_acc, fc_acc, proj_acc, *, blocks, parts
):
    step = pl.program_id(0)
    width = x_ref.shape[1]

    @pl.when(step == 0)
    def _():
        out_acc[...] = jnp.zeros_like(out_acc)
        fc_acc[...] = jnp.zeros_like(fc_acc)
        proj_acc[...] = jnp.zeros_like(proj_acc)
        d_vec[...] = jnp.zeros_like(d_vec)

    @pl.when(step < blocks)
    def _():
        att = att_ref[...]
        go = go_ref[...]
        middle = x_ref[...].astype(f32) + mm(att, w_out[...])
        unit, inverse = row_stats(middle)
        second = (unit * gain[...] + bias[...]).astype(bf16)
        res = middle
        back = jnp.zeros_like(middle)
        chunk = w_fc.shape[1] // parts
        for c in range(parts):
            cols = slice(c * chunk, (c + 1) * chunk)
            pre = mm(second, w_fc[:, cols])
            square = pre * pre
            t = jnp.tanh(gelu_in * pre * (1.0 + gelu_cube * square))
            rise = 0.5 * (1.0 + t)
            hidden = (pre * rise).astype(bf16)
            slope = rise + pre * (1.0 - t * t) * (0.5 * gelu_in + (1.5 * gelu_in * gelu_cube) * square)
            res = res + mm(hidden, w_proj[cols, :])
            pre_grad = (mm(go, w_proj[cols, :], NT) * slope).astype(bf16)
            back = back + mm(pre_grad, w_fc[:, cols], NT)
            proj_acc[c] += mm(hidden, go, TN)
            fc_acc[c] += mm(second, pre_grad, TN)
        res_ref[...] = res.astype(bf16)
        d_vec[0:1, :] += jnp.sum(back * unit, axis=0, keepdims=True)
        d_vec[1:2, :] += jnp.sum(back, axis=0, keepdims=True)
        mid_grad = go.astype(f32) + pull_norm(back, unit, inverse, gain[...])
        mid_ref[...] = mid_grad
        branch = mid_grad.astype(bf16)
        ctx_ref[...] = mm(branch, w_out[...], NT).astype(bf16)
        out_acc[...] += mm(att, branch, TN).reshape(out_acc.shape)

    @pl.when(step >= blocks)
    def _():
        part = step - blocks
        d_out[...] = out_acc[part].astype(bf16)
        d_fc[...] = fc_acc[part].astype(bf16)
        d_proj[...] = proj_acc[part].astype(bf16)


def middle_rows(inputs, attended, out_rows, gain, bias, w_out, w_fc, w_proj, rows):
    total_rows, width = inputs.shape
    hidden = w_fc.shape[1]
    blocks = total_rows // rows
    parts = 4
    chunk, share = hidden // parts, width // parts
    whole = lambda shape: pl.BlockSpec(shape, lambda i: (0, 0), pipeline_mode=pl.Buffered(1))
    block = pl.BlockSpec((rows, width), lambda i: (jnp.minimum(i, blocks - 1), 0))
    late = lambda i: jnp.maximum(i - blocks, 0)
    macs = total_rows * width * (6 * hidden + 3 * width)
    return pl.pallas_call(
        partial(middle_kernel, blocks=blocks, parts=parts),
        grid=(blocks + parts,),
        in_specs=[
            block,
            block,
            block,
            whole((1, width)),
            whole((1, width)),
            whole(w_out.shape),
            whole(w_fc.shape),
            whole(w_proj.shape),
        ],
        out_specs=[
            block,
            block,
            block,
            pl.BlockSpec((share, width), lambda i: (late(i), 0)),
            pl.BlockSpec((width, chunk), lambda i: (late(i), 0)),
            pl.BlockSpec((chunk, width), lambda i: (late(i), 0)),
            pl.BlockSpec((8, width), lambda i: (0, 0)),
        ],
        out_shape=[
            jax.ShapeDtypeStruct((total_rows, width), bf16),
            jax.ShapeDtypeStruct((total_rows, width), f32),
            jax.ShapeDtypeStruct((total_rows, width), bf16),
            jax.ShapeDtypeStruct(w_out.shape, bf16),
            jax.ShapeDtypeStruct((parts * width, chunk), bf16),
            jax.ShapeDtypeStruct(w_proj.shape, bf16),
            jax.ShapeDtypeStruct((8, width), f32),
        ],
        scratch_shapes=[
            pltpu.VMEM((parts, share, width), f32),
            pltpu.VMEM((parts, width, chunk), f32),
            pltpu.VMEM((parts, chunk, width), f32),
        ],
        compiler_params=pltpu.CompilerParams(vmem_limit_bytes=60 * 2**20),
        cost_estimate=pl.CostEstimate(
            flops=2 * macs, transcendentals=total_rows * hidden, bytes_accessed=60 * 2**20
        ),
        name="middle_rows",
    )(inputs, attended, out_rows, gain[None], bias[None], w_out, w_fc, w_proj)


def last_kernel(
    pos, x_ref, mid_ref, d_ref, gain, w_ref, cot_ref, high_ref, low_ref, *refs, skip
):
    out_ref, d_vec = refs[skip : skip + 2]

    @pl.when(pl.program_id(0) == 0)
    def _():
        d_vec[...] = jnp.zeros_like(d_vec)

    width = x_ref.shape[1]
    up = mm(high_ref[...], cot_ref[...]) + mm(low_ref[...], cot_ref[...])
    for c in range(3):
        up = up + mm(d_ref[c], w_ref[:, c * width : (c + 1) * width], NT)
    unit, inverse = row_stats(x_ref[...].astype(f32))
    d_vec[0:1, :] += jnp.sum(up * unit, axis=0, keepdims=True)
    d_vec[1:2, :] += jnp.sum(up, axis=0, keepdims=True)
    out_ref[...] = (mid_ref[...] + pull_norm(up, unit, inverse, gain[...])).astype(bf16)


def last_rows(inputs, middle_grad, dqkv, gain, w_qkv, mem_cot, tables, slot_pos, rows, parts):
    total_rows, width = inputs.shape
    basis = tables[0].shape[1]
    whole = lambda shape: pl.BlockSpec(shape, lambda i, pos: (0, 0), pipeline_mode=pl.Buffered(1))
    block = pl.BlockSpec((rows, width), lambda i, pos: (i, 0))
    ridge = pl.BlockSpec((rows, basis), lambda i, pos: (pos[i], 0))
    outputs = pl.pallas_call(
        partial(last_kernel, skip=len(parts)),
        grid_spec=pltpu.PrefetchScalarGridSpec(
            num_scalar_prefetch=1,
            grid=(total_rows // rows,),
            in_specs=[
                block,
                block,
                pl.BlockSpec((3, rows, width), lambda i, pos: (0, i, 0)),
                whole((1, width)),
                whole(w_qkv.shape),
                whole(mem_cot.shape),
                ridge,
                ridge,
            ]
            + [pl.BlockSpec(memory_space=pl.ANY)] * len(parts),
            out_specs=[block, pl.BlockSpec((8, width), lambda i, pos: (0, 0))]
            + [pl.BlockSpec(memory_space=pl.ANY)] * len(parts),
        ),
        out_shape=[
            jax.ShapeDtypeStruct((total_rows, width), bf16),
            jax.ShapeDtypeStruct((8, width), f32),
        ]
        + [jax.ShapeDtypeStruct(part.shape, part.dtype) for part in parts],
        input_output_aliases={9 + c: c + 2 for c in range(len(parts))},
        compiler_params=pltpu.CompilerParams(vmem_limit_bytes=40 * 2**20),
        cost_estimate=pl.CostEstimate(
            flops=2 * total_rows * width * (3 * width + 2 * basis),
            transcendentals=0,
            bytes_accessed=16 * total_rows * width + 2 * w_qkv.size,
        ),
        name="last_rows",
    )(slot_pos, inputs, middle_grad, dqkv, gain[None], w_qkv, mem_cot, *tables, *parts)
    return outputs[:2], outputs[2:]


def density_of(queries, u_mu, u_sig, basis_count):
    highest = lax.Precision.HIGHEST
    centres = (jnp.arange(basis_count, dtype=f32) + 0.5) / basis_count
    width_b = 0.75 / basis_count
    wide = queries.astype(f32)
    centre = jax.nn.sigmoid(jnp.einsum("qhd,hd->qh", wide, u_mu, precision=highest))
    spread = spread_var * jax.nn.softplus(
        jnp.einsum("qhd,hd->qh", wide, u_sig, precision=highest)
    )
    spread = (spread + spread_floor)[..., None]
    offset = centre[..., None] - centres
    return width_b * lax.rsqrt(spread) * jnp.exp(-offset * offset / (2.0 * spread))


def spread_attend(projected, mem_kv, u_mu, u_sig, q_pos, k_pos, team, flag, heads):
    rows, width = projected.shape[0], projected.shape[1] // 3
    basis = mem_kv.shape[0]
    head = width // heads
    scale = 1.0 / math.sqrt(head)
    shape = (-1, heads, head)
    queries = projected[:, :width].reshape(shape)
    both = lax.all_gather(projected[:, width:], "blk", axis=0, tiled=True, axis_index_groups=team)
    keys, values = both[:, :width].reshape(shape), both[:, width:].reshape(shape)
    scores = jnp.einsum("qhd,khd->hqk", queries, keys, preferred_element_type=f32) * scale
    allowed = (q_pos[:, None] >= k_pos[None, :])[None]
    scores = jnp.where(allowed, scores, masked_value)
    lse = jax.nn.logsumexp(scores, axis=-1, keepdims=True)
    probs = jnp.where(allowed, jnp.exp(scores - lse), 0.0)
    local = jnp.einsum("hqk,khd->qhd", probs.astype(bf16), values, preferred_element_type=f32)
    mem_values = mem_kv[:, width:].reshape(shape)
    density = density_of(queries, u_mu, u_sig, basis).astype(bf16)
    mem = jnp.einsum("qhn,nhd->qhd", density, mem_values, preferred_element_type=f32)
    attended = (local + flag.astype(f32) * mem).astype(bf16).reshape(rows, width)
    return attended, (queries, keys, values, probs, local, density, mem_values)


def spread_back(kept, context_grad, u_mu, u_sig, team, flag):
    queries, keys, values, probs, local, density, mem_values = kept
    rows, heads, head = queries.shape
    basis = mem_values.shape[0]
    scale = 1.0 / math.sqrt(head)
    g = context_grad.reshape(queries.shape)
    term = jnp.sum(g.astype(f32) * local, axis=-1)
    dv = jnp.einsum("hqk,qhd->khd", probs.astype(bf16), g, preferred_element_type=f32)
    dp = jnp.einsum("qhd,khd->hqk", g, values, preferred_element_type=f32)
    ds = (probs * (dp - term.T[..., None])).astype(bf16)
    dq = jnp.einsum("hqk,khd->qhd", ds, keys, preferred_element_type=f32) * scale
    dk = jnp.einsum("hqk,qhd->khd", ds, queries, preferred_element_type=f32) * scale
    both = jnp.stack([dk.reshape(-1, heads * head), dv.reshape(-1, heads * head)], 1).astype(bf16)
    both = lax.psum_scatter(both, "blk", scatter_dimension=0, tiled=True, axis_index_groups=team)
    g_on = g * flag.astype(bf16)
    pull = jnp.einsum("qhd,nhd->qhn", g_on, mem_values, preferred_element_type=f32)
    dmv = jnp.einsum("qhn,qhd->nhd", density, g_on, preferred_element_type=f32)
    dq_mem, d_mu, d_sig = jax.vjp(
        lambda q, m, s: density_of(q, m, s, basis), queries.astype(f32), u_mu, u_sig
    )[1](pull)
    dqkv = jnp.stack([(dq + dq_mem).reshape(rows, -1).astype(bf16), both[:, 0], both[:, 1]])
    return dqkv, dmv.reshape(basis, -1), d_mu.reshape(1, -1), d_sig.reshape(1, -1)


def per_device(
    tokens,
    memory,
    present,
    block_pos,
    ln1_gain,
    ln1_bias,
    w_qkv,
    w_out,
    ln2_gain,
    ln2_bias,
    w_fc,
    w_proj,
    w_mu,
    w_sig,
    grad_out,
    grad_memory,
):
    members, seg_rows, model_width = tokens.shape
    blocks = lax.axis_size("blk")
    teams = blocks // members
    heads, basis = w_mu.shape
    head = model_width // heads
    total_rows = members * seg_rows
    seg_len = seg_rows * blocks
    scale = 1.0 / math.sqrt(head)
    rank = lax.axis_index("blk")
    member, team_rank = rank % members, rank // members
    team = [[s + members * j for j in range(teams)] for s in range(members)]

    token_slots = collect_blocks(tokens, members)
    token_slots, grad_out = lax.optimization_barrier((token_slots, grad_out))
    grad_slots = collect_blocks(grad_out, members)
    inputs_low = jnp.concatenate(token_slots, axis=0)
    mem = pick(memory, member)
    mem_cot = pick(grad_memory, member)
    flag = lax.dynamic_slice_in_dim(present, member, 1, 0)
    on = flag[0].astype(f32)
    seg_order = pick(block_pos, member)
    back = (member - jnp.arange(members, dtype=jnp.int32)) % members
    slot_pos = seg_order[team_rank * members + back]

    ridge_table, carry_table = memory_tables(basis, seg_len)
    ridge_parts = [jnp.asarray(part) for part in split_low(ridge_table)]
    ridge_turned = [jnp.asarray(part) for part in split_low(ridge_table.T)]
    carry_parts = [jnp.asarray(part) for part in split_low(carry_table)]

    normed_low, projected, gathered = front(
        inputs_low, ln1_gain, ln1_bias, w_qkv, ridge_parts, slot_pos, seg_rows
    )
    mem_kv = mm(mem, w_qkv[:, model_width:]).astype(bf16)
    mem_keys = mem_kv[:, :model_width].astype(f32)
    wide_mu = jnp.repeat(w_mu.T, head, axis=1)
    wide_sig = jnp.repeat(w_sig.T, head, axis=1)
    u_mu = scale * jnp.sum(mem_keys * wide_mu, axis=0)
    u_sig = scale * jnp.sum(mem_keys * wide_sig, axis=0)

    if teams > 1:
        gathered = lax.psum(gathered, "blk", axis_index_groups=team)
    new_memory = (on * sum(mm(part, mem) for part in carry_parts) + gathered).astype(bf16)

    if teams == 1:
        order = jnp.argmax(
            slot_pos[None, :] == jnp.arange(members, dtype=jnp.int32)[:, None], axis=1
        ).astype(jnp.int32)
        u_cols = jnp.concatenate(
            [u_mu[:, None], u_sig[:, None], jnp.zeros((model_width, 6), f32)], axis=1
        )
        attended, local, lse = attend_segment(projected, mem_kv, u_cols, order, flag, members, head)
    else:
        row_ids = jnp.arange(seg_rows, dtype=jnp.int32)
        q_pos = (slot_pos[:, None] * seg_rows + row_ids[None, :]).reshape(-1)
        key_order = seg_order.reshape(teams, members)[:, back]
        k_pos = (key_order[:, :, None] * seg_rows + row_ids).reshape(-1)
        mu_heads, sig_heads = u_mu.reshape(heads, head), u_sig.reshape(heads, head)
        attended, kept = spread_attend(
            projected, mem_kv, mu_heads, sig_heads, q_pos, k_pos, team, flag, heads
        )
    new_memory = share_segments(new_memory, members)

    out_rows = jnp.concatenate(grad_slots, axis=0)
    result_rows, middle_grad, context_grad, d_out, d_fc, d_proj, ln2_grads = middle_rows(
        inputs_low, attended, out_rows, ln2_gain, ln2_bias, w_out, w_fc, w_proj,
        min(256, total_rows),
    )
    result_back = ReturnBlocks(result_rows, members)
    proj_sum = WeightSum(d_proj, ("core", "x", "y", "z"))
    fc_sum = WeightSum(d_fc, ("core", "y", "x", "z"))

    def qkv_part(first, last):
        cols = slice(first, last)
        parts = [mm(normed_low, dqkv[0, :, cols], TN)]
        parts.append(mm(normed_low, dqkv[1, :, cols], TN))
        parts.append(mm(normed_low, dqkv[2, :, cols], TN))
        mem_grads = (mem_keys_part(cols), mem_values_grad[:, cols])
        for c in range(2):
            parts[c + 1] = parts[c + 1] + mm(mem_once, mem_grads[c], TN)
        return jnp.concatenate([part.astype(bf16) for part in parts], axis=1)

    def mem_keys_part(cols):
        part = wide_mu[:, cols] * mu_sum[:, cols] + wide_sig[:, cols] * sig_sum[:, cols]
        return part.astype(bf16)

    mem_once = mem * (team_rank == 0).astype(bf16)
    if teams == 1:
        kept = None
        moves = [proj_sum, fc_sum]
        pairs = model_width // LANES
        early = 2 * pairs // 3
        for pair in range(pairs):
            now = moves + [result_back] if pair == 1 else moves
            kept = beside(
                now,
                lambda parts: attend_back(
                    pair, kept, projected, mem_kv, u_cols, context_grad, local, lse, order, flag,
                    members, head, parts
                ),
            )
            if pair == early - 1:
                dqkv, mem_values_grad, pulls = kept
                mu_sum, sig_sum = scale * pulls[0:1], scale * pulls[1:2]
                qkv_early = qkv_part(0, early * LANES)
                first_sum = WeightSum(
                    jnp.concatenate([d_out, qkv_early], axis=1), ("core", "x", "y", "z")
                )
                moves.append(first_sum)
        dqkv, mem_values_grad, pulls = kept
        mu_sum, sig_sum = scale * pulls[0:1], scale * pulls[1:2]
        mu_part, sig_part = mu_sum, sig_sum
        split = early * LANES
    else:
        dqkv, mem_values_grad, mu_part, sig_part = spread_back(
            kept, context_grad, mu_heads, sig_heads, team, flag
        )
        mu_part, sig_part = scale * mu_part, scale * sig_part
        mem_values_grad, mu_sum, sig_sum = lax.psum(
            (mem_values_grad, mu_part, sig_part), "blk", axis_index_groups=team
        )
        mem_values_grad = mem_values_grad.astype(bf16)
        split = model_width // 2
        qkv_early = qkv_part(0, split)
        first_sum = WeightSum(
            jnp.concatenate([d_out, qkv_early], axis=1), ("core", "x", "y", "z")
        )
        moves = [proj_sum, fc_sum, first_sum]
    result = result_back.finish()
    late_sum = WeightSum(qkv_part(split, model_width), ("core", "x", "y", "z"))

    token_grad, ln1_grads = beside(
        moves + [late_sum],
        lambda parts: last_rows(
            inputs_low, middle_grad, dqkv, ln1_gain, w_qkv, mem_cot, ridge_turned, slot_pos, seg_rows, parts
        ),
    )
    grad_tokens = ReturnBlocks(token_grad, members).finish()
    mem_keys_grad = mem_keys_part(slice(None))
    w_mu_grad = jnp.sum((mem_keys * mu_part).reshape(basis, heads, head), axis=2).T
    w_sig_grad = jnp.sum((mem_keys * sig_part).reshape(basis, heads, head), axis=2).T
    memory_grad = (
        on
        * (
            mm(mem_keys_grad, w_qkv[:, model_width : 2 * model_width], NT)
            + mm(mem_values_grad, w_qkv[:, 2 * model_width :], NT)
            + sum(mm(part, mem_cot, TN) for part in carry_parts)
        )
    ).astype(bf16)
    memory_grad = share_segments(memory_grad, members)

    first, late = first_sum.finish().astype(f32), late_sum.finish().astype(f32)
    w_out_grad = first[:, :model_width]
    rest = model_width - split
    w_qkv_grad = jnp.concatenate(
        [
            piece
            for c in range(3)
            for piece in (
                first[:, model_width + c * split : model_width + (c + 1) * split],
                late[:, c * rest : (c + 1) * rest],
            )
        ],
        axis=1,
    )
    w_proj_grad = proj_sum.finish().astype(f32)
    fc_chunks = fc_sum.finish().reshape(-1, model_width, w_fc.shape[1] * model_width // fc_sum.block.shape[0])
    w_fc_grad = jnp.concatenate([part.astype(f32) for part in fc_chunks], axis=1)

    vectors = jnp.concatenate(
        [ln1_grads[:2].reshape(-1), ln2_grads[:2].reshape(-1), w_mu_grad.reshape(-1), w_sig_grad.reshape(-1)]
    )
    vectors = sum_all(vectors.reshape(-1, LANES)).reshape(-1)
    ln1_gain_grad, ln1_bias_grad, ln2_gain_grad, ln2_bias_grad = [
        vectors[c * model_width : (c + 1) * model_width] for c in range(4)
    ]
    tail = vectors[4 * model_width :].reshape(2, heads, basis)
    w_mu_grad, w_sig_grad = tail[0], tail[1]
    return (
        result,
        new_memory,
        grad_tokens,
        memory_grad,
        ln1_gain_grad,
        ln1_bias_grad,
        w_qkv_grad,
        w_out_grad,
        ln2_gain_grad,
        ln2_bias_grad,
        w_fc_grad,
        w_proj_grad,
        w_mu_grad,
        w_sig_grad,
    )


def solution(mesh):
    split = P("seg", "blk", None)
    whole_seg = P("seg", None, None)
    return jax.shard_map(
        per_device,
        mesh=mesh,
        in_specs=(split, whole_seg, P("seg"), P("seg", None)) + (P(),) * 10 + (split, whole_seg),
        out_specs=(split, whole_seg, split, whole_seg) + (P(),) * 10,
        check_vma=False,
    )
```

```python
from functools import partial
import math

import jax
import jax.numpy as jnp
import ml_dtypes
import numpy as np
from jax import lax
from jax.experimental import pallas as pl
from jax.experimental.pallas import tpu as pltpu
from jax.sharding import PartitionSpec as P

eps_norm = 1e-05
ridge_weight = 1.0
contract = 0.5
spread_var = 0.05
spread_floor = 0.002
masked_value = -1e30
LANES = 128
f32 = jnp.float32
bf16 = jnp.bfloat16

NN = (((1,), (0,)), ((), ()))
NT = (((1,), (1,)), ((), ()))
TN = (((0,), (0,)), ((), ()))


def mm(a, b, dims=NN):
    return lax.dot_general(a, b, dims, preferred_element_type=f32)


def basis_table(points, basis_count):
    centres = (np.arange(basis_count, dtype=np.float64) + 0.5) / basis_count
    width_b = 0.75 / basis_count
    offset = points[..., None] - centres
    return np.exp(-offset * offset / (2.0 * width_b * width_b))


def split_low(table):
    high_part = table.astype(ml_dtypes.bfloat16)
    low_part = (table - high_part.astype(np.float64)).astype(ml_dtypes.bfloat16)
    return high_part, low_part


def memory_tables(basis_count, seg_len):
    samples = (np.arange(basis_count, dtype=np.float64) + 0.5) / basis_count
    squeezed = basis_table(contract * samples, basis_count)
    stretched = basis_table(samples, basis_count)
    carry_map = squeezed.T @ stretched
    times = contract + (1.0 - contract) * (np.arange(seg_len, dtype=np.float64) + 0.5) / seg_len
    all_times = basis_table(times, basis_count)
    gram = squeezed.T @ squeezed + all_times.T @ all_times + ridge_weight * np.eye(basis_count)
    return np.linalg.solve(gram, all_times.T), np.linalg.solve(gram, carry_map)


def digit_route(size, stride, radix, distance):
    route = []
    for i in range(size):
        digit = (i // stride) % radix
        route.append((i, i + ((digit + distance) % radix - digit) * stride))
    return route


def pick(stack, index):
    return lax.dynamic_index_in_dim(stack, index, 0, keepdims=False)


def put(stack, block, index):
    return lax.dynamic_update_index_in_dim(stack, block, index, 0)


def sum_step(block, axis, stride, radix):
    size = lax.axis_size(axis)
    total = block.astype(f32)
    for distance in range(1, radix):
        total = total + lax.ppermute(block, axis, digit_route(size, stride, radix, distance)).astype(f32)
    return total.astype(block.dtype)


def gather_step(block, axis, stride, radix):
    size = lax.axis_size(axis)
    digit = (lax.axis_index(axis) // stride) % radix
    if radix == 1:
        return block[None]
    stack = jnp.zeros((radix,) + block.shape, block.dtype)
    stack = put(stack, block, digit)
    for distance in range(1, radix):
        got = lax.ppermute(block, axis, digit_route(size, stride, radix, distance))
        stack = put(stack, got, (digit - distance) % radix)
    return stack


def near(size):
    return 2 if size % 2 == 0 else 1


def sum_all(block):
    for axis in ("blk", "seg"):
        size, stride = lax.axis_size(axis), 1
        while stride < size:
            radix = near(size // stride)
            radix = size // stride if radix == 1 else radix
            block = sum_step(block, axis, stride, radix)
            stride *= radix
    return block


def source_of(member, distance, members):
    return member ^ distance if members & (members - 1) == 0 else (member - distance) % members


def target_of(member, distance, members):
    return member ^ distance if members & (members - 1) == 0 else (member + distance) % members


def member_route(members, distance, find):
    size = lax.axis_size("blk")
    return [(i, i - i % members + find(i % members, distance, members)) for i in range(size)]


def collect_blocks(stack, members):
    member = lax.axis_index("blk") % members
    slots = [pick(stack, member)]
    for distance in range(1, members):
        sent = pick(stack, target_of(member, distance, members))
        slots.append(lax.ppermute(sent, "blk", member_route(members, distance, target_of)))
    return slots


def return_blocks(rows, members):
    member = lax.axis_index("blk") % members
    slots = rows.reshape((members, -1) + rows.shape[1:])
    stack = jnp.zeros(slots.shape, slots.dtype)
    stack = put(stack, slots[0], member)
    for distance in range(1, members):
        got = lax.ppermute(slots[distance], "blk", member_route(members, distance, source_of))
        stack = put(stack, got, target_of(member, distance, members))
    return stack


def share_segments(block, members):
    if members % 2 == 0:
        stack = gather_step(block, "blk", 2, members // 2)
        stack = gather_step(stack, "blk", 1, 2)
        return jnp.swapaxes(stack, 0, 1).reshape((members,) + block.shape)
    return gather_step(block, "blk", 1, members)


def spread_parts(centre_arg, spread_arg):
    centre = 1.0 / (1.0 + jnp.exp(-centre_arg))
    tail = jnp.exp(-jnp.abs(spread_arg))
    spread = spread_var * (jnp.maximum(spread_arg, 0.0) + jnp.log(1.0 + tail)) + spread_floor
    return centre, spread


def forward_kernel(
    order, flag, q_ref, k_ref, v_ref, mv_ref, ut_ref, att_ref, loc_ref, lse_ref, vt, *, rows, count, head, scale
):
    lane = lax.broadcasted_iota(jnp.int32, (1, LANES), 1)
    sel_scale = [jnp.where(lane // head == a, scale, 0.0).astype(bf16) for a in range(2)]
    basis = mv_ref.shape[0]
    centres = (lax.broadcasted_iota(jnp.int32, (basis, 1), 0).astype(f32) + 0.5) / basis
    width_b = 0.75 / basis
    on = flag[0].astype(f32)
    half = rows // 2
    mv_t = mv_ref[...].astype(f32).T.astype(bf16)
    ones = jnp.ones((head, rows), bf16)

    def turn(j, _):
        here = pl.ds(pl.multiple_of(j * rows, rows), rows)
        v_t = v_ref[here, :].astype(f32).T.astype(bf16)
        vt[0, :, here] = jnp.concatenate([v_t[:head, :], ones], axis=0)
        vt[1, :, here] = jnp.concatenate([ones, v_t[head:, :]], axis=0)
        return 0

    lax.fori_loop(0, count, turn, 0)

    def absorb(carry, qs, k, v_t, masked):
        out = []
        for a in range(2):
            top, acc = carry[2 * a], carry[2 * a + 1]
            s = mm(k, qs[a], NT)
            if masked:
                key_id = lax.broadcasted_iota(jnp.int32, s.shape, 0)
                s = jnp.where(lax.broadcasted_iota(jnp.int32, s.shape, 1) >= key_id, s, masked_value)
            new_top = jnp.maximum(top, jnp.max(s, axis=0, keepdims=True))
            p = jnp.exp(s - new_top)
            acc = acc * jnp.exp(top - new_top) + mm(v_t[a], p.astype(bf16))
            out += [new_top, acc]
        return tuple(out)

    def q_step(i, _):
        at = pl.multiple_of(order[i] * rows, rows)
        q = q_ref[pl.ds(at, rows), :]
        qs = [q * s for s in sel_scale]
        start = (jnp.full((1, rows), masked_value, f32), jnp.zeros((LANES, rows), f32)) * 2

        def tile(j, carry):
            kat = pl.multiple_of(order[j] * rows, rows)
            v_t = [vt[a, :, pl.ds(kat, rows)] for a in range(2)]
            return absorb(carry, qs, k_ref[pl.ds(kat, rows), :], v_t, False)

        carry = lax.fori_loop(0, i, tile, start)
        k = k_ref[pl.ds(at, half), :]
        v_t = [vt[a, :, pl.ds(at, half)] for a in range(2)]
        carry = absorb(carry, qs, k, v_t, True)
        at_late = pl.multiple_of(at + half, half)
        k = k_ref[pl.ds(at_late, half), :]
        v_t = [vt[a, :, pl.ds(at_late, half)] for a in range(2)]
        late = absorb(tuple(c[:, half:] for c in carry), [x[half:] for x in qs], k, v_t, True)
        carry = [jnp.concatenate([c[:, :half], d], axis=1) for c, d in zip(carry, late)]
        here = pl.ds(pl.multiple_of(i * rows, rows), rows)
        total = [carry[1][head : head + 1, :], carry[3][0:1, :]]
        local = jnp.concatenate([carry[1][:head] / total[0], carry[3][head:] / total[1]], axis=0)
        for a in range(2):
            lse_ref[0, a : a + 1, here] = carry[2 * a] + jnp.log(total[a])
        q_t = q.astype(f32).T
        toward_mu = q_t * ut_ref[:, 0:1]
        toward_sig = q_t * ut_ref[:, 1:2]
        mem = []
        for a in range(2):
            lo, hi = a * head, (a + 1) * head
            centre_arg = jnp.sum(toward_mu[lo:hi], axis=0, keepdims=True)
            spread_arg = jnp.sum(toward_sig[lo:hi], axis=0, keepdims=True)
            centre, spread = spread_parts(centre_arg, spread_arg)
            offset = centre - centres
            density = jnp.exp(offset * offset * (-0.5 / spread)) * (width_b * lax.rsqrt(spread))
            mem.append(mm(mv_t[lo:hi], density.astype(bf16)))
        loc_ref[pl.ds(at, rows), :] = local.T
        att_ref[pl.ds(at, rows), :] = (local + on * jnp.concatenate(mem, axis=0)).T.astype(bf16)
        return 0

    lax.fori_loop(0, count, q_step, 0)


def backward_kernel(
    order, flag, q_ref, k_ref, v_ref, mv_ref, ut_ref, g_ref, loc_ref, lse_ref, *refs,
    rows, count, head, scale, skip
):
    dqkv_ref, dmv_ref, da_ref = refs[skip : skip + 3]
    dq_acc, kt, term, dmv_acc, da_acc = refs[-5:]
    lane = lax.broadcasted_iota(jnp.int32, (1, LANES), 1)
    inside = [lane // head == a for a in range(2)]
    sel = [jnp.where(m, 1.0, 0.0).astype(bf16) for m in inside]
    sel_scale = [jnp.where(m, scale, 0.0).astype(bf16) for m in inside]
    basis = mv_ref.shape[0]
    centres = (lax.broadcasted_iota(jnp.int32, (basis, 1), 0).astype(f32) + 0.5) / basis
    width_b = 0.75 / basis
    on = jnp.full((1, LANES), flag[0].astype(f32)).astype(bf16)
    half = rows // 2
    dmv_acc[...] = jnp.zeros_like(dmv_acc)
    da_acc[...] = jnp.zeros_like(da_acc)

    def mem_step(i, _):
        at = pl.multiple_of(order[i] * rows, rows)
        here = pl.ds(pl.multiple_of(i * rows, rows), rows)
        q = q_ref[pl.ds(at, rows), :]
        g = g_ref[pl.ds(at, rows), :]
        kt[:, pl.ds(at, rows)] = (k_ref[pl.ds(at, rows), :].astype(f32) * scale).T.astype(bf16)
        term_t = (g.astype(f32) * loc_ref[pl.ds(at, rows), :]).T
        qt = q.astype(f32).T
        toward_mu = qt * ut_ref[:, 0:1]
        toward_sig = qt * ut_ref[:, 1:2]
        g_on = g * on
        pulls = []
        for a in range(2):
            lo, hi = a * head, (a + 1) * head
            term[a : a + 1, here] = jnp.sum(term_t[lo:hi, :], axis=0, keepdims=True)
            centre_arg = jnp.sum(toward_mu[lo:hi, :], axis=0, keepdims=True)
            spread_arg = jnp.sum(toward_sig[lo:hi, :], axis=0, keepdims=True)
            centre, spread = spread_parts(centre_arg, spread_arg)
            offset = centre - centres
            square = offset * offset
            density = jnp.exp(square * (-0.5 / spread)) * (width_b * lax.rsqrt(spread))
            ga = g_on * sel[a]
            pull = mm(mv_ref[...] * sel[a], g_on, NT) * density
            dmv_acc[...] += mm(density.astype(bf16), ga)
            sum0 = jnp.sum(pull, axis=0, keepdims=True)
            sum1 = jnp.sum(pull * offset, axis=0, keepdims=True)
            sum2 = jnp.sum(pull * square, axis=0, keepdims=True)
            d_centre = -sum1 / spread * centre * (1.0 - centre)
            d_spread = (sum2 / spread - sum0) * (0.5 * spread_var) / spread
            d_spread = d_spread / (1.0 + jnp.exp(-spread_arg))
            pulls += [d_centre, d_spread]
            dq_acc[lo:hi, here] = ut_ref[lo:hi, 0:1] * d_centre + ut_ref[lo:hi, 1:2] * d_spread
        stacked = jnp.concatenate(pulls + [jnp.zeros((4, rows), f32)], axis=0)
        high_part = stacked.astype(bf16)
        low_part = (stacked - high_part.astype(f32)).astype(bf16)
        da_acc[...] += mm(high_part, q) + mm(low_part, q)
        return 0

    lax.fori_loop(0, count, mem_step, 0)
    dmv_ref[...] = dmv_acc[...].astype(bf16)
    row8 = lax.broadcasted_iota(jnp.int32, (8, LANES), 0)
    da = da_acc[...]
    mu_row = jnp.where(inside[0], da[0:1, :], da[2:3, :])
    sig_row = jnp.where(inside[0], da[1:2, :], da[3:4, :])
    da_ref[...] = jnp.where(row8 == 0, mu_row, sig_row)

    def pull_tile(dk, dv, ks, vs, kat, qat, here, size_k, size_q, masked):
        q = q_ref[pl.ds(qat, size_q), :]
        g = g_ref[pl.ds(qat, size_q), :]
        for a in range(2):
            lo, hi = a * head, (a + 1) * head
            s = mm(ks[a], q, NT)
            p = jnp.exp(s - lse_ref[0, a : a + 1, here])
            if masked:
                key_id = lax.broadcasted_iota(jnp.int32, s.shape, 0)
                p = jnp.where(lax.broadcasted_iota(jnp.int32, s.shape, 1) >= key_id, p, 0.0)
            ds = (p * (mm(vs[a], g, NT) - term[a : a + 1, here])).astype(bf16)
            dv = dv + mm(p.astype(bf16), g * sel[a])
            dk = dk + mm(ds, q * sel_scale[a])
            dq_acc[lo:hi, here] += mm(kt[lo:hi, pl.ds(kat, size_k)], ds)
        return dk, dv

    def k_step(j, _):
        at = pl.multiple_of(order[j] * rows, rows)
        k = k_ref[pl.ds(at, rows), :]
        v = v_ref[pl.ds(at, rows), :]
        ks = [k * s for s in sel_scale]
        vs = [v * s for s in sel]
        zero = jnp.zeros((half, LANES), f32)
        here = pl.multiple_of(j * rows, rows)
        early = pull_tile(
            zero, zero, [x[:half] for x in ks], [x[:half] for x in vs], at, at,
            pl.ds(here, rows), half, rows, True
        )
        at_late = pl.multiple_of(at + half, half)
        late = pull_tile(
            zero, zero, [x[half:] for x in ks], [x[half:] for x in vs], at_late, at_late,
            pl.ds(pl.multiple_of(here + half, half), half), half, half, True
        )
        carry = tuple(jnp.concatenate([x, y], axis=0) for x, y in zip(early, late))

        def tile(i, carry):
            qat = pl.multiple_of(order[i] * rows, rows)
            there = pl.ds(pl.multiple_of(i * rows, rows), rows)
            return pull_tile(carry[0], carry[1], ks, vs, at, qat, there, rows, rows, False)

        dk, dv = lax.fori_loop(j + 1, count, tile, carry)
        dqkv_ref[1, pl.ds(at, rows), :] = dk.astype(bf16)
        dqkv_ref[2, pl.ds(at, rows), :] = dv.astype(bf16)
        return 0

    lax.fori_loop(0, count, k_step, 0)

    def q_out(i, _):
        at = pl.multiple_of(order[i] * rows, rows)
        here = pl.ds(pl.multiple_of(i * rows, rows), rows)
        dqkv_ref[0, pl.ds(at, rows), :] = dq_acc[:, here].T.astype(bf16)
        return 0

    lax.fori_loop(0, count, q_out, 0)


def attend_segment(projected, mem_kv, u_cols, order, flag, count, head):
    total_rows = projected.shape[0]
    width = projected.shape[1] // 3
    basis = mem_kv.shape[0]
    pairs = width // LANES
    rows = total_rows // count
    scale = 1.0 / math.sqrt(head)

    def column(base):
        return pl.BlockSpec((total_rows, LANES), lambda h, *_: (0, base + h))

    tiles = total_rows * (total_rows + rows) // 2 * 2 * pairs
    return pl.pallas_call(
        partial(forward_kernel, rows=rows, count=count, head=head, scale=scale),
        grid_spec=pltpu.PrefetchScalarGridSpec(
            num_scalar_prefetch=2,
            grid=(pairs,),
            in_specs=[
                column(0),
                column(pairs),
                column(2 * pairs),
                pl.BlockSpec((basis, LANES), lambda h, *_: (0, pairs + h)),
                pl.BlockSpec((LANES, 8), lambda h, *_: (h, 0)),
            ],
            out_specs=[
                column(0),
                column(0),
                pl.BlockSpec((1, 2, total_rows), lambda h, *_: (h, 0, 0)),
            ],
            scratch_shapes=[pltpu.VMEM((2, LANES, total_rows), bf16)],
        ),
        out_shape=[
            jax.ShapeDtypeStruct((total_rows, width), bf16),
            jax.ShapeDtypeStruct((total_rows, width), f32),
            jax.ShapeDtypeStruct((pairs, 2, total_rows), f32),
        ],
        compiler_params=pltpu.CompilerParams(vmem_limit_bytes=48 * 2**20),
        cost_estimate=pl.CostEstimate(
            flops=tiles * 4 * 256, transcendentals=tiles, bytes_accessed=12 * total_rows * width
        ),
        name="attend_forward",
    )(order, flag, projected, projected, projected, mem_kv, u_cols)


def attend_back(pair, kept, projected, mem_kv, u_cols, context_grad, local, lse, order, flag, count, head, waits):
    total_rows = projected.shape[0]
    width = projected.shape[1] // 3
    basis = mem_kv.shape[0]
    pairs = width // LANES
    rows = total_rows // count
    scale = 1.0 / math.sqrt(head)

    def column(base):
        return pl.BlockSpec((total_rows, LANES), lambda h, *_: (0, base + pair))

    tiles = total_rows * (total_rows + rows) // 2 * 2
    kept = list(kept) if kept is not None else []
    extra = kept + list(waits)
    return pl.pallas_call(
        partial(backward_kernel, rows=rows, count=count, head=head, scale=scale, skip=len(extra)),
        grid_spec=pltpu.PrefetchScalarGridSpec(
            num_scalar_prefetch=2,
            grid=(1,),
            in_specs=[
                column(0),
                column(pairs),
                column(2 * pairs),
                pl.BlockSpec((basis, LANES), lambda h, *_: (0, pairs + pair)),
                pl.BlockSpec((LANES, 8), lambda h, *_: (pair, 0)),
                column(0),
                column(0),
                pl.BlockSpec((1, 2, total_rows), lambda h, *_: (pair, 0, 0)),
            ]
            + [pl.BlockSpec(memory_space=pl.ANY)] * len(extra),
            out_specs=[
                pl.BlockSpec((3, total_rows, LANES), lambda h, *_: (0, 0, pair)),
                pl.BlockSpec((basis, LANES), lambda h, *_: (0, pair)),
                pl.BlockSpec((8, LANES), lambda h, *_: (0, pair)),
            ],
            scratch_shapes=[
                pltpu.VMEM((LANES, total_rows), f32),
                pltpu.VMEM((LANES, total_rows), bf16),
                pltpu.VMEM((8, total_rows), f32),
                pltpu.VMEM((basis, LANES), f32),
                pltpu.VMEM((8, LANES), f32),
            ],
        ),
        out_shape=[
            jax.ShapeDtypeStruct((3, total_rows, width), bf16),
            jax.ShapeDtypeStruct((basis, width), bf16),
            jax.ShapeDtypeStruct((8, width), f32),
        ],
        input_output_aliases={10 + c: c for c in range(len(kept))},
        compiler_params=pltpu.CompilerParams(vmem_limit_bytes=48 * 2**20),
        cost_estimate=pl.CostEstimate(
            flops=tiles, transcendentals=0, bytes_accessed=2 * total_rows * LANES
        ),
        name=f"attend_backward_{pair}",
    )(
        order, flag, projected, projected, projected, mem_kv, u_cols, context_grad, local, lse, *extra
    )


def row_stats(values):
    centred = values - jnp.mean(values, axis=-1, keepdims=True)
    inverse = lax.rsqrt(jnp.mean(centred * centred, axis=-1, keepdims=True) + eps_norm)
    return centred * inverse, inverse


def pull_norm(upstream, unit_rows, inverse, gain_vec):
    scaled = upstream * gain_vec
    return inverse * (
        scaled
        - jnp.mean(scaled, axis=-1, keepdims=True)
        - unit_rows * jnp.mean(scaled * unit_rows, axis=-1, keepdims=True)
    )


def front_kernel(pos, x_ref, gain, bias, w_ref, high_ref, low_ref, *refs, kept):
    copy_ref, normed_ref, proj_ref, sum_ref = refs[-4:]
    copy_ref[...] = x_ref[...]
    unit, _ = row_stats(x_ref[...].astype(f32))
    normed = (unit * gain[...] + bias[...]).astype(bf16)
    normed_ref[...] = normed
    width = normed.shape[1]
    for c in range(3):
        cols = slice(c * width, (c + 1) * width)
        proj_ref[:, cols] = mm(normed, w_ref[:, cols]).astype(bf16)

    @pl.when(pl.program_id(0) == 0)
    def _():
        sum_ref[...] = refs[0][...] if kept else jnp.zeros_like(sum_ref)

    sum_ref[...] += mm(high_ref[...], normed) + mm(low_ref[...], normed)


def front(inputs, base, total_rows, kept, gain, bias, w_qkv, tables, slot_pos, rows):
    width = inputs.shape[1]
    basis = tables[0].shape[0]
    count = inputs.shape[0] // rows
    whole = lambda shape: pl.BlockSpec(shape, lambda i, pos: (0, 0), pipeline_mode=pl.Buffered(1))
    ridge = pl.BlockSpec((basis, rows), lambda i, pos: (0, pos[base + i]))
    block = pl.BlockSpec((rows, width), lambda i, pos: (base + i, 0))
    kept = list(kept[3:]) + list(kept[:3]) if kept is not None else []
    kept_specs = [whole((basis, width))] + [pl.BlockSpec(memory_space=pl.ANY)] * 3 if kept else []
    return pl.pallas_call(
        partial(front_kernel, kept=bool(kept)),
        grid_spec=pltpu.PrefetchScalarGridSpec(
            num_scalar_prefetch=1,
            grid=(count,),
            in_specs=[
                pl.BlockSpec((rows, width), lambda i, pos: (i, 0)),
                whole((1, width)),
                whole((1, width)),
                whole(w_qkv.shape),
                ridge,
                ridge,
            ]
            + kept_specs,
            out_specs=[
                block,
                block,
                pl.BlockSpec((rows, 3 * width), lambda i, pos: (base + i, 0)),
                pl.BlockSpec((basis, width), lambda i, pos: (0, 0)),
            ],
        ),
        out_shape=[
            jax.ShapeDtypeStruct((total_rows, width), bf16),
            jax.ShapeDtypeStruct((total_rows, width), bf16),
            jax.ShapeDtypeStruct((total_rows, 3 * width), bf16),
            jax.ShapeDtypeStruct((basis, width), f32),
        ],
        input_output_aliases={8 + c: c for c in range(3)} if kept else {},
        compiler_params=pltpu.CompilerParams(vmem_limit_bytes=40 * 2**20),
        cost_estimate=pl.CostEstimate(
            flops=2 * count * rows * width * (3 * width + 2 * basis),
            transcendentals=0,
            bytes_accessed=10 * count * rows * width + 2 * w_qkv.size,
        ),
        name=f"front_{base}",
    )(slot_pos, inputs, gain[None], bias[None], w_qkv, *tables, *kept)


gelu_in = math.sqrt(2.0 / math.pi)
gelu_cube = 0.044715


def middle_kernel(
    x_ref, att_ref, go_ref, gain, bias, w_out, w_fc, w_proj,
    res_ref, mid_ref, ctx_ref, d_all, d_vec, out_acc, fc_acc, proj_acc, *, blocks, parts
):
    step = pl.program_id(0)
    width = x_ref.shape[1]

    @pl.when(step == 0)
    def _():
        out_acc[...] = jnp.zeros_like(out_acc)
        fc_acc[...] = jnp.zeros_like(fc_acc)
        proj_acc[...] = jnp.zeros_like(proj_acc)
        d_vec[...] = jnp.zeros_like(d_vec)

    @pl.when(step < blocks)
    def _():
        att = att_ref[...]
        go = go_ref[...]
        middle = x_ref[...].astype(f32) + mm(att, w_out[...])
        unit, inverse = row_stats(middle)
        second = (unit * gain[...] + bias[...]).astype(bf16)
        res = middle
        back = jnp.zeros_like(middle)
        chunk = w_fc.shape[1] // parts
        for c in range(parts):
            cols = slice(c * chunk, (c + 1) * chunk)
            pre = mm(second, w_fc[:, cols])
            square = pre * pre
            t = jnp.tanh(gelu_in * pre * (1.0 + gelu_cube * square))
            rise = 0.5 * (1.0 + t)
            hidden = (pre * rise).astype(bf16)
            slope = rise + pre * (1.0 - t * t) * (0.5 * gelu_in + (1.5 * gelu_in * gelu_cube) * square)
            res = res + mm(hidden, w_proj[cols, :])
            pre_grad = (mm(go, w_proj[cols, :], NT) * slope).astype(bf16)
            back = back + mm(pre_grad, w_fc[:, cols], NT)
            proj_acc[c] += mm(hidden, go, TN)
            fc_acc[c] += mm(second, pre_grad, TN)
        res_ref[...] = res.astype(bf16)
        d_vec[0:1, :] += jnp.sum(back * unit, axis=0, keepdims=True)
        d_vec[1:2, :] += jnp.sum(back, axis=0, keepdims=True)
        mid_grad = go.astype(f32) + pull_norm(back, unit, inverse, gain[...])
        mid_ref[...] = mid_grad
        branch = mid_grad.astype(bf16)
        ctx_ref[...] = mm(branch, w_out[...], NT).astype(bf16)
        out_acc[...] += mm(att, branch, TN).reshape(out_acc.shape)

    @pl.when(step >= blocks)
    def _():
        part = step - blocks
        chunk = proj_acc.shape[1]
        d_all[:width, :] = fc_acc[part].astype(bf16)
        d_all[width : width + chunk, :] = proj_acc[part].astype(bf16)
        d_all[width + chunk :, :] = out_acc[part].astype(bf16)


def middle_rows(inputs, attended, out_rows, gain, bias, w_out, w_fc, w_proj, rows):
    total_rows, width = inputs.shape
    hidden = w_fc.shape[1]
    blocks = total_rows // rows
    parts = hidden // width
    chunk, share = hidden // parts, width // parts
    whole = lambda shape: pl.BlockSpec(shape, lambda i: (0, 0), pipeline_mode=pl.Buffered(1))
    block = pl.BlockSpec((rows, width), lambda i: (jnp.minimum(i, blocks - 1), 0))
    late = lambda i: jnp.maximum(i - blocks, 0)
    macs = total_rows * width * (6 * hidden + 3 * width)
    return pl.pallas_call(
        partial(middle_kernel, blocks=blocks, parts=parts),
        grid=(blocks + parts,),
        in_specs=[
            block,
            block,
            block,
            whole((1, width)),
            whole((1, width)),
            whole(w_out.shape),
            whole(w_fc.shape),
            whole(w_proj.shape),
        ],
        out_specs=[
            block,
            block,
            block,
            pl.BlockSpec((width + chunk + share, width), lambda i: (late(i), 0)),
            pl.BlockSpec((8, width), lambda i: (0, 0)),
        ],
        out_shape=[
            jax.ShapeDtypeStruct((total_rows, width), bf16),
            jax.ShapeDtypeStruct((total_rows, width), f32),
            jax.ShapeDtypeStruct((total_rows, width), bf16),
            jax.ShapeDtypeStruct((parts * (width + chunk + share), width), bf16),
            jax.ShapeDtypeStruct((8, width), f32),
        ],
        scratch_shapes=[
            pltpu.VMEM((parts, share, width), f32),
            pltpu.VMEM((parts, width, chunk), f32),
            pltpu.VMEM((parts, chunk, width), f32),
        ],
        compiler_params=pltpu.CompilerParams(vmem_limit_bytes=60 * 2**20),
        cost_estimate=pl.CostEstimate(
            flops=2 * macs, transcendentals=total_rows * hidden, bytes_accessed=60 * 2**20
        ),
        name="middle_rows",
    )(inputs, attended, out_rows, gain[None], bias[None], w_out, w_fc, w_proj)


def last_kernel(
    pos, x_ref, mid_ref, d_ref, gain, w_ref, cot_ref, high_ref, low_ref, *refs
):
    out_ref, d_vec = refs[-2:]

    @pl.when(pl.program_id(0) == 0)
    def _():
        d_vec[...] = jnp.zeros_like(d_vec)

    width = x_ref.shape[1]
    up = mm(high_ref[...], cot_ref[...]) + mm(low_ref[...], cot_ref[...])
    for c in range(3):
        up = up + mm(d_ref[c], w_ref[:, c * width : (c + 1) * width], NT)
    unit, inverse = row_stats(x_ref[...].astype(f32))
    d_vec[0:1, :] += jnp.sum(up * unit, axis=0, keepdims=True)
    d_vec[1:2, :] += jnp.sum(up, axis=0, keepdims=True)
    out_ref[...] = (mid_ref[...] + pull_norm(up, unit, inverse, gain[...])).astype(bf16)


def last_rows(inputs, middle_grad, dqkv, gain, w_qkv, mem_cot, tables, slot_pos, rows, waits):
    total_rows, width = inputs.shape
    basis = tables[0].shape[1]
    whole = lambda shape: pl.BlockSpec(shape, lambda i, pos: (0, 0), pipeline_mode=pl.Buffered(1))
    block = pl.BlockSpec((rows, width), lambda i, pos: (i, 0))
    ridge = pl.BlockSpec((rows, basis), lambda i, pos: (pos[i], 0))
    return pl.pallas_call(
        last_kernel,
        grid_spec=pltpu.PrefetchScalarGridSpec(
            num_scalar_prefetch=1,
            grid=(total_rows // rows,),
            in_specs=[
                block,
                block,
                pl.BlockSpec((3, rows, width), lambda i, pos: (0, i, 0)),
                whole((1, width)),
                whole(w_qkv.shape),
                whole(mem_cot.shape),
                ridge,
                ridge,
            ]
            + [pl.BlockSpec(memory_space=pl.ANY)] * len(waits),
            out_specs=[block, pl.BlockSpec((8, width), lambda i, pos: (0, 0))],
        ),
        out_shape=[
            jax.ShapeDtypeStruct((total_rows, width), bf16),
            jax.ShapeDtypeStruct((8, width), f32),
        ],
        compiler_params=pltpu.CompilerParams(vmem_limit_bytes=40 * 2**20),
        cost_estimate=pl.CostEstimate(
            flops=2 * total_rows * width * (3 * width + 2 * basis),
            transcendentals=0,
            bytes_accessed=16 * total_rows * width + 2 * w_qkv.size,
        ),
        name="last_rows",
    )(slot_pos, inputs, middle_grad, dqkv, gain[None], w_qkv, mem_cot, *tables, *waits)


def density_of(queries, u_mu, u_sig, basis_count):
    highest = lax.Precision.HIGHEST
    centres = (jnp.arange(basis_count, dtype=f32) + 0.5) / basis_count
    width_b = 0.75 / basis_count
    wide = queries.astype(f32)
    centre = jax.nn.sigmoid(jnp.einsum("qhd,hd->qh", wide, u_mu, precision=highest))
    spread = spread_var * jax.nn.softplus(
        jnp.einsum("qhd,hd->qh", wide, u_sig, precision=highest)
    )
    spread = (spread + spread_floor)[..., None]
    offset = centre[..., None] - centres
    return width_b * lax.rsqrt(spread) * jnp.exp(-offset * offset / (2.0 * spread))


def spread_attend(projected, mem_kv, u_mu, u_sig, q_pos, k_pos, team, flag, heads):
    rows, width = projected.shape[0], projected.shape[1] // 3
    basis = mem_kv.shape[0]
    head = width // heads
    scale = 1.0 / math.sqrt(head)
    shape = (-1, heads, head)
    queries = projected[:, :width].reshape(shape)
    both = lax.all_gather(projected[:, width:], "blk", axis=0, tiled=True, axis_index_groups=team)
    keys, values = both[:, :width].reshape(shape), both[:, width:].reshape(shape)
    scores = jnp.einsum("qhd,khd->hqk", queries, keys, preferred_element_type=f32) * scale
    allowed = (q_pos[:, None] >= k_pos[None, :])[None]
    scores = jnp.where(allowed, scores, masked_value)
    lse = jax.nn.logsumexp(scores, axis=-1, keepdims=True)
    probs = jnp.where(allowed, jnp.exp(scores - lse), 0.0)
    local = jnp.einsum("hqk,khd->qhd", probs.astype(bf16), values, preferred_element_type=f32)
    mem_values = mem_kv[:, width:].reshape(shape)
    density = density_of(queries, u_mu, u_sig, basis).astype(bf16)
    mem = jnp.einsum("qhn,nhd->qhd", density, mem_values, preferred_element_type=f32)
    attended = (local + flag.astype(f32) * mem).astype(bf16).reshape(rows, width)
    return attended, (queries, keys, values, probs, local, density, mem_values)


def spread_back(kept, context_grad, u_mu, u_sig, team, flag):
    queries, keys, values, probs, local, density, mem_values = kept
    rows, heads, head = queries.shape
    basis = mem_values.shape[0]
    scale = 1.0 / math.sqrt(head)
    g = context_grad.reshape(queries.shape)
    term = jnp.sum(g.astype(f32) * local, axis=-1)
    dv = jnp.einsum("hqk,qhd->khd", probs.astype(bf16), g, preferred_element_type=f32)
    dp = jnp.einsum("qhd,khd->hqk", g, values, preferred_element_type=f32)
    ds = (probs * (dp - term.T[..., None])).astype(bf16)
    dq = jnp.einsum("hqk,khd->qhd", ds, keys, preferred_element_type=f32) * scale
    dk = jnp.einsum("hqk,qhd->khd", ds, queries, preferred_element_type=f32) * scale
    both = jnp.stack([dk.reshape(-1, heads * head), dv.reshape(-1, heads * head)], 1).astype(bf16)
    both = lax.psum_scatter(both, "blk", scatter_dimension=0, tiled=True, axis_index_groups=team)
    g_on = g * flag.astype(bf16)
    pull = jnp.einsum("qhd,nhd->qhn", g_on, mem_values, preferred_element_type=f32)
    dmv = jnp.einsum("qhn,qhd->nhd", density, g_on, preferred_element_type=f32)
    dq_mem, d_mu, d_sig = jax.vjp(
        lambda q, m, s: density_of(q, m, s, basis), queries.astype(f32), u_mu, u_sig
    )[1](pull)
    dqkv = jnp.stack([(dq + dq_mem).reshape(rows, -1).astype(bf16), both[:, 0], both[:, 1]])
    return dqkv, dmv.reshape(basis, -1), d_mu.reshape(1, -1), d_sig.reshape(1, -1)


def per_device(
    tokens,
    memory,
    present,
    block_pos,
    ln1_gain,
    ln1_bias,
    w_qkv,
    w_out,
    ln2_gain,
    ln2_bias,
    w_fc,
    w_proj,
    w_mu,
    w_sig,
    grad_out,
    grad_memory,
):
    members, seg_rows, model_width = tokens.shape
    blocks = lax.axis_size("blk")
    teams = blocks // members
    heads, basis = w_mu.shape
    head = model_width // heads
    total_rows = members * seg_rows
    seg_len = seg_rows * blocks
    scale = 1.0 / math.sqrt(head)
    rank = lax.axis_index("blk")
    member, team_rank = rank % members, rank // members
    team = [[s + members * j for j in range(teams)] for s in range(members)]

    token_slots = collect_blocks(tokens, members)
    token_slots, grad_out = lax.optimization_barrier((token_slots, grad_out))
    grad_slots = collect_blocks(grad_out, members)
    mem = pick(memory, member)
    mem_cot = pick(grad_memory, member)
    flag = lax.dynamic_slice_in_dim(present, member, 1, 0)
    on = flag[0].astype(f32)
    seg_order = pick(block_pos, member)
    back = source_of(member, jnp.arange(members, dtype=jnp.int32), members)
    slot_pos = seg_order[team_rank * members + back]

    ridge_table, carry_table = memory_tables(basis, seg_len)
    ridge_parts = [jnp.asarray(part) for part in split_low(ridge_table)]
    ridge_turned = [jnp.asarray(part) for part in split_low(ridge_table.T)]
    carry_parts = [jnp.asarray(part) for part in split_low(carry_table)]

    begun = None
    near_slots = near(members)
    for first, last in ((0, near_slots), (near_slots, members)):
        if first < last:
            begun = front(
                jnp.concatenate(token_slots[first:last], axis=0), first, total_rows, begun,
                ln1_gain, ln1_bias, w_qkv, ridge_parts, slot_pos, seg_rows,
            )
    inputs_low, normed_low, projected, gathered = begun
    mem_kv = mm(mem, w_qkv[:, model_width:]).astype(bf16)
    mem_keys = mem_kv[:, :model_width].astype(f32)
    wide_mu = jnp.repeat(w_mu.T, head, axis=1)
    wide_sig = jnp.repeat(w_sig.T, head, axis=1)
    u_mu = scale * jnp.sum(mem_keys * wide_mu, axis=0)
    u_sig = scale * jnp.sum(mem_keys * wide_sig, axis=0)

    if teams > 1:
        gathered = lax.psum(gathered, "blk", axis_index_groups=team)
    new_memory = (on * sum(mm(part, mem) for part in carry_parts) + gathered).astype(bf16)

    if teams == 1:
        order = jnp.argmax(
            slot_pos[None, :] == jnp.arange(members, dtype=jnp.int32)[:, None], axis=1
        ).astype(jnp.int32)
        u_cols = jnp.concatenate(
            [u_mu[:, None], u_sig[:, None], jnp.zeros((model_width, 6), f32)], axis=1
        )
        attended, local, lse = attend_segment(projected, mem_kv, u_cols, order, flag, members, head)
    else:
        row_ids = jnp.arange(seg_rows, dtype=jnp.int32)
        q_pos = (slot_pos[:, None] * seg_rows + row_ids[None, :]).reshape(-1)
        key_order = seg_order.reshape(teams, members)[:, back]
        k_pos = (key_order[:, :, None] * seg_rows + row_ids).reshape(-1)
        mu_heads, sig_heads = u_mu.reshape(heads, head), u_sig.reshape(heads, head)
        attended, kept = spread_attend(
            projected, mem_kv, mu_heads, sig_heads, q_pos, k_pos, team, flag, heads
        )
    new_memory = share_segments(new_memory, members)

    out_rows = jnp.concatenate(grad_slots, axis=0)
    result_rows, middle_grad, context_grad, d_all, ln2_grads = middle_rows(
        inputs_low, attended, out_rows, ln2_gain, ln2_bias, w_out, w_fc, w_proj,
        min(256, total_rows),
    )
    result = return_blocks(result_rows, members)
    everyone = ("seg", "blk")
    all_sum = lax.psum(d_all, everyone)

    def qkv_part(first, last):
        cols = slice(first, last)
        parts = [mm(normed_low, dqkv[0, :, cols], TN)]
        parts.append(mm(normed_low, dqkv[1, :, cols], TN))
        parts.append(mm(normed_low, dqkv[2, :, cols], TN))
        mem_grads = (mem_keys_part(cols), mem_values_grad[:, cols])
        for c in range(2):
            parts[c + 1] = parts[c + 1] + mm(mem_once, mem_grads[c], TN)
        return jnp.concatenate([part.astype(bf16) for part in parts], axis=1)

    def mem_keys_part(cols):
        part = wide_mu[:, cols] * mu_sum[:, cols] + wide_sig[:, cols] * sig_sum[:, cols]
        return part.astype(bf16)

    mem_once = mem * (team_rank == 0).astype(bf16)
    if teams == 1:
        kept = None
        pairs = model_width // LANES
        for pair in range(pairs):
            kept = attend_back(
                pair, kept, projected, mem_kv, u_cols, context_grad, local, lse, order, flag,
                members, head, [result, new_memory] if pair == pairs - 2 else [],
            )
        dqkv, mem_values_grad, pulls = kept
        mu_sum, sig_sum = scale * pulls[0:1], scale * pulls[1:2]
        mu_part, sig_part = mu_sum, sig_sum
    else:
        dqkv, mem_values_grad, mu_part, sig_part = spread_back(
            kept, context_grad, mu_heads, sig_heads, team, flag
        )
        mu_part, sig_part = scale * mu_part, scale * sig_part
        mem_values_grad, mu_sum, sig_sum = lax.psum(
            (mem_values_grad, mu_part, sig_part), "blk", axis_index_groups=team
        )
        mem_values_grad = mem_values_grad.astype(bf16)
    qkv_sum = lax.psum(qkv_part(0, model_width), ("blk", "seg"))

    token_grad, ln1_grads = last_rows(
        inputs_low, middle_grad, dqkv, ln1_gain, w_qkv, mem_cot, ridge_turned, slot_pos, seg_rows, []
    )
    grad_tokens = return_blocks(token_grad, members)
    mem_keys_grad = mem_keys_part(slice(None))
    w_mu_grad = jnp.sum((mem_keys * mu_part).reshape(basis, heads, head), axis=2).T
    w_sig_grad = jnp.sum((mem_keys * sig_part).reshape(basis, heads, head), axis=2).T
    memory_grad = (
        on
        * (
            mm(mem_keys_grad, w_qkv[:, model_width : 2 * model_width], NT)
            + mm(mem_values_grad, w_qkv[:, 2 * model_width :], NT)
            + sum(mm(part, mem_cot, TN) for part in carry_parts)
        )
    ).astype(bf16)
    memory_grad = share_segments(memory_grad, members)

    w_qkv_grad = qkv_sum.astype(f32)
    parts = w_fc.shape[1] // model_width
    pieces = all_sum.reshape(parts, -1, model_width).astype(f32)
    w_fc_grad = jnp.concatenate([pieces[c, :model_width] for c in range(parts)], axis=1)
    w_proj_grad = pieces[:, model_width : 2 * model_width].reshape(w_proj.shape)
    w_out_grad = pieces[:, 2 * model_width :].reshape(w_out.shape)

    vectors = jnp.concatenate(
        [ln1_grads[:2].reshape(-1), ln2_grads[:2].reshape(-1), w_mu_grad.reshape(-1), w_sig_grad.reshape(-1)]
    )
    vectors = sum_all(vectors.reshape(-1, LANES)).reshape(-1)
    ln1_gain_grad, ln1_bias_grad, ln2_gain_grad, ln2_bias_grad = [
        vectors[c * model_width : (c + 1) * model_width] for c in range(4)
    ]
    tail = vectors[4 * model_width :].reshape(2, heads, basis)
    w_mu_grad, w_sig_grad = tail[0], tail[1]
    return (
        result,
        new_memory,
        grad_tokens,
        memory_grad,
        ln1_gain_grad,
        ln1_bias_grad,
        w_qkv_grad,
        w_out_grad,
        ln2_gain_grad,
        ln2_bias_grad,
        w_fc_grad,
        w_proj_grad,
        w_mu_grad,
        w_sig_grad,
    )


def solution(mesh):
    split = P("seg", "blk", None)
    whole_seg = P("seg", None, None)
    return jax.shard_map(
        per_device,
        mesh=mesh,
        in_specs=(split, whole_seg, P("seg"), P("seg", None)) + (P(),) * 10 + (split, whole_seg),
        out_specs=(split, whole_seg, split, whole_seg) + (P(),) * 10,
        check_vma=False,
    )
```

```python
from functools import partial
import math

import jax
import jax.numpy as jnp
import ml_dtypes
import numpy as np
from jax import lax
from jax.experimental import pallas as pl
from jax.experimental.pallas import tpu as pltpu
from jax.sharding import PartitionSpec as P

eps_norm = 1e-05
ridge_weight = 1.0
contract = 0.5
spread_var = 0.05
spread_floor = 0.002
masked_value = -1e30
LANES = 128
f32 = jnp.float32
bf16 = jnp.bfloat16

NN = (((1,), (0,)), ((), ()))
NT = (((1,), (1,)), ((), ()))
TN = (((0,), (0,)), ((), ()))


def mm(a, b, dims=NN):
    return lax.dot_general(a, b, dims, preferred_element_type=f32)


def basis_table(points, basis_count):
    centres = (np.arange(basis_count, dtype=np.float64) + 0.5) / basis_count
    width_b = 0.75 / basis_count
    offset = points[..., None] - centres
    return np.exp(-offset * offset / (2.0 * width_b * width_b))


def split_low(table):
    high_part = table.astype(ml_dtypes.bfloat16)
    low_part = (table - high_part.astype(np.float64)).astype(ml_dtypes.bfloat16)
    return high_part, low_part


def memory_tables(basis_count, seg_len):
    samples = (np.arange(basis_count, dtype=np.float64) + 0.5) / basis_count
    squeezed = basis_table(contract * samples, basis_count)
    stretched = basis_table(samples, basis_count)
    carry_map = squeezed.T @ stretched
    times = contract + (1.0 - contract) * (np.arange(seg_len, dtype=np.float64) + 0.5) / seg_len
    all_times = basis_table(times, basis_count)
    gram = squeezed.T @ squeezed + all_times.T @ all_times + ridge_weight * np.eye(basis_count)
    return np.linalg.solve(gram, all_times.T), np.linalg.solve(gram, carry_map)


def digit_route(size, stride, radix, distance):
    route = []
    for i in range(size):
        digit = (i // stride) % radix
        route.append((i, i + ((digit + distance) % radix - digit) * stride))
    return route


def pick(stack, index):
    return lax.dynamic_index_in_dim(stack, index, 0, keepdims=False)


def put(stack, block, index):
    return lax.dynamic_update_index_in_dim(stack, block, index, 0)


def digit_of(name):
    blk, seg = lax.axis_size("blk"), lax.axis_size("seg")
    core, side = near(blk), near(seg)
    return {
        "core": ("blk", 1, core),
        "y": ("blk", core, blk // core),
        "x": ("seg", 1, side),
        "z": ("seg", side, seg // side),
    }[name]


def send_parts(terms, name, mark=0):
    axis, stride, radix = digit_of(name)
    size = lax.axis_size(axis)
    digit = (lax.axis_index(axis) // stride) % radix + mark
    stacks = [term.reshape(radix, -1, term.shape[1]) for term in terms]

    def part(index):
        return sum(pick(stack, index).astype(f32) for stack in stacks).astype(bf16)

    got = [
        lax.ppermute(part((digit + distance) % radix), axis, digit_route(size, stride, radix, distance))
        for distance in range(1, radix)
    ]
    return part(digit), got


def send_whole(block, name):
    axis, stride, radix = digit_of(name)
    size = lax.axis_size(axis)
    return [
        lax.ppermute(block, axis, digit_route(size, stride, radix, distance))
        for distance in range(1, radix)
    ]


def place(own, got, name, mark=0):
    axis, stride, radix = digit_of(name)
    digit = (lax.axis_index(axis) // stride) % radix + mark
    parts = [own] + got
    if radix == 2:
        return jnp.where(digit == 0, jnp.concatenate(parts), jnp.concatenate(parts[::-1]))
    return jnp.concatenate(
        [
            lax.select_n((digit - k) % radix, *parts) if radix > 1 else own
            for k in range(radix)
        ]
    )


def sum_step(block, axis, stride, radix):
    size = lax.axis_size(axis)
    total = block.astype(f32)
    for distance in range(1, radix):
        total = total + lax.ppermute(block, axis, digit_route(size, stride, radix, distance)).astype(f32)
    return total.astype(block.dtype)


def gather_step(block, axis, stride, radix):
    size = lax.axis_size(axis)
    digit = (lax.axis_index(axis) // stride) % radix
    if radix == 1:
        return block[None]
    stack = jnp.zeros((radix,) + block.shape, block.dtype)
    stack = put(stack, block, digit)
    for distance in range(1, radix):
        got = lax.ppermute(block, axis, digit_route(size, stride, radix, distance))
        stack = put(stack, got, (digit - distance) % radix)
    return stack


def near(size):
    return 2 if size % 2 == 0 else 1


def sum_all(block):
    for axis in ("blk", "seg"):
        size, stride = lax.axis_size(axis), 1
        while stride < size:
            radix = near(size // stride)
            radix = size // stride if radix == 1 else radix
            block = sum_step(block, axis, stride, radix)
            stride *= radix
    return block


def source_of(member, distance, members):
    return member ^ distance if members & (members - 1) == 0 else (member - distance) % members


def target_of(member, distance, members):
    return member ^ distance if members & (members - 1) == 0 else (member + distance) % members


def member_route(members, distance, find):
    size = lax.axis_size("blk")
    return [(i, i - i % members + find(i % members, distance, members)) for i in range(size)]


def collect_blocks(stack, members):
    member = lax.axis_index("blk") % members
    slots = [pick(stack, member)]
    for distance in range(1, members):
        sent = pick(stack, target_of(member, distance, members))
        slots.append(lax.ppermute(sent, "blk", member_route(members, distance, target_of)))
    return slots


def return_slot(slots, distance, members):
    return lax.ppermute(slots[distance], "blk", member_route(members, distance, source_of))


def place_blocks(parts, members, mark=0):
    member = lax.axis_index("blk") % members + mark
    stack = jnp.zeros((members,) + parts[0].shape, parts[0].dtype)
    for distance, part in enumerate(parts):
        stack = put(stack, part, target_of(member, distance, members))
    return stack


def share_segments(block, members):
    if members % 2 == 0:
        stack = gather_step(block, "blk", 2, members // 2)
        stack = gather_step(stack, "blk", 1, 2)
        return jnp.swapaxes(stack, 0, 1).reshape((members,) + block.shape)
    return gather_step(block, "blk", 1, members)


def spread_parts(centre_arg, spread_arg):
    centre = 1.0 / (1.0 + jnp.exp(-centre_arg))
    tail = jnp.exp(-jnp.abs(spread_arg))
    spread = spread_var * (jnp.maximum(spread_arg, 0.0) + jnp.log(1.0 + tail)) + spread_floor
    return centre, spread


def forward_kernel(
    order, flag, q_ref, k_ref, v_ref, mv_ref, ut_ref, att_ref, loc_ref, lse_ref, vt, *, rows, count, head, scale
):
    lane = lax.broadcasted_iota(jnp.int32, (1, LANES), 1)
    sel_scale = [jnp.where(lane // head == a, scale, 0.0).astype(bf16) for a in range(2)]
    basis = mv_ref.shape[0]
    centres = (lax.broadcasted_iota(jnp.int32, (basis, 1), 0).astype(f32) + 0.5) / basis
    width_b = 0.75 / basis
    on = flag[0].astype(f32)
    half = rows // 2
    mv_t = mv_ref[...].astype(f32).T.astype(bf16)
    ones = jnp.ones((head, rows), bf16)

    def turn(j, _):
        here = pl.ds(pl.multiple_of(j * rows, rows), rows)
        v_t = v_ref[here, :].astype(f32).T.astype(bf16)
        vt[0, :, here] = jnp.concatenate([v_t[:head, :], ones], axis=0)
        vt[1, :, here] = jnp.concatenate([ones, v_t[head:, :]], axis=0)
        return 0

    lax.fori_loop(0, count, turn, 0)

    def absorb(carry, qs, k, v_t, masked):
        out = []
        for a in range(2):
            top, acc = carry[2 * a], carry[2 * a + 1]
            s = mm(k, qs[a], NT)
            if masked:
                key_id = lax.broadcasted_iota(jnp.int32, s.shape, 0)
                s = jnp.where(lax.broadcasted_iota(jnp.int32, s.shape, 1) >= key_id, s, masked_value)
            new_top = jnp.maximum(top, jnp.max(s, axis=0, keepdims=True))
            p = jnp.exp(s - new_top)
            acc = acc * jnp.exp(top - new_top) + mm(v_t[a], p.astype(bf16))
            out += [new_top, acc]
        return tuple(out)

    def q_step(i, _):
        at = pl.multiple_of(order[i] * rows, rows)
        q = q_ref[pl.ds(at, rows), :]
        qs = [q * s for s in sel_scale]
        start = (jnp.full((1, rows), masked_value, f32), jnp.zeros((LANES, rows), f32)) * 2

        def tile(j, carry):
            kat = pl.multiple_of(order[j] * rows, rows)
            v_t = [vt[a, :, pl.ds(kat, rows)] for a in range(2)]
            return absorb(carry, qs, k_ref[pl.ds(kat, rows), :], v_t, False)

        carry = lax.fori_loop(0, i, tile, start)
        k = k_ref[pl.ds(at, half), :]
        v_t = [vt[a, :, pl.ds(at, half)] for a in range(2)]
        carry = absorb(carry, qs, k, v_t, True)
        at_late = pl.multiple_of(at + half, half)
        k = k_ref[pl.ds(at_late, half), :]
        v_t = [vt[a, :, pl.ds(at_late, half)] for a in range(2)]
        late = absorb(tuple(c[:, half:] for c in carry), [x[half:] for x in qs], k, v_t, True)
        carry = [jnp.concatenate([c[:, :half], d], axis=1) for c, d in zip(carry, late)]
        here = pl.ds(pl.multiple_of(i * rows, rows), rows)
        total = [carry[1][head : head + 1, :], carry[3][0:1, :]]
        local = jnp.concatenate([carry[1][:head] / total[0], carry[3][head:] / total[1]], axis=0)
        for a in range(2):
            lse_ref[0, a : a + 1, here] = carry[2 * a] + jnp.log(total[a])
        q_t = q.astype(f32).T
        toward_mu = q_t * ut_ref[:, 0:1]
        toward_sig = q_t * ut_ref[:, 1:2]
        mem = []
        for a in range(2):
            lo, hi = a * head, (a + 1) * head
            centre_arg = jnp.sum(toward_mu[lo:hi], axis=0, keepdims=True)
            spread_arg = jnp.sum(toward_sig[lo:hi], axis=0, keepdims=True)
            centre, spread = spread_parts(centre_arg, spread_arg)
            offset = centre - centres
            density = jnp.exp(offset * offset * (-0.5 / spread)) * (width_b * lax.rsqrt(spread))
            mem.append(mm(mv_t[lo:hi], density.astype(bf16)))
        loc_ref[pl.ds(at, rows), :] = local.T
        att_ref[pl.ds(at, rows), :] = (local + on * jnp.concatenate(mem, axis=0)).T.astype(bf16)
        return 0

    lax.fori_loop(0, count, q_step, 0)


def backward_kernel(
    order, flag, q_ref, k_ref, v_ref, mv_ref, ut_ref, g_ref, loc_ref, lse_ref, *refs,
    rows, count, head, scale, skip
):
    dqkv_ref, dmv_ref, da_ref = refs[skip : skip + 3]
    dq_acc, kt, term, dmv_acc, da_acc = refs[-5:]
    lane = lax.broadcasted_iota(jnp.int32, (1, LANES), 1)
    inside = [lane // head == a for a in range(2)]
    sel = [jnp.where(m, 1.0, 0.0).astype(bf16) for m in inside]
    sel_scale = [jnp.where(m, scale, 0.0).astype(bf16) for m in inside]
    basis = mv_ref.shape[0]
    centres = (lax.broadcasted_iota(jnp.int32, (basis, 1), 0).astype(f32) + 0.5) / basis
    width_b = 0.75 / basis
    on = jnp.full((1, LANES), flag[0].astype(f32)).astype(bf16)
    half = rows // 2
    dmv_acc[...] = jnp.zeros_like(dmv_acc)
    da_acc[...] = jnp.zeros_like(da_acc)

    def mem_step(i, _):
        at = pl.multiple_of(order[i] * rows, rows)
        here = pl.ds(pl.multiple_of(i * rows, rows), rows)
        q = q_ref[pl.ds(at, rows), :]
        g = g_ref[pl.ds(at, rows), :]
        kt[:, pl.ds(at, rows)] = (k_ref[pl.ds(at, rows), :].astype(f32) * scale).T.astype(bf16)
        term_t = (g.astype(f32) * loc_ref[pl.ds(at, rows), :]).T
        qt = q.astype(f32).T
        toward_mu = qt * ut_ref[:, 0:1]
        toward_sig = qt * ut_ref[:, 1:2]
        g_on = g * on
        pulls = []
        for a in range(2):
            lo, hi = a * head, (a + 1) * head
            term[a : a + 1, here] = jnp.sum(term_t[lo:hi, :], axis=0, keepdims=True)
            centre_arg = jnp.sum(toward_mu[lo:hi, :], axis=0, keepdims=True)
            spread_arg = jnp.sum(toward_sig[lo:hi, :], axis=0, keepdims=True)
            centre, spread = spread_parts(centre_arg, spread_arg)
            offset = centre - centres
            square = offset * offset
            density = jnp.exp(square * (-0.5 / spread)) * (width_b * lax.rsqrt(spread))
            ga = g_on * sel[a]
            pull = mm(mv_ref[...] * sel[a], g_on, NT) * density
            dmv_acc[...] += mm(density.astype(bf16), ga)
            sum0 = jnp.sum(pull, axis=0, keepdims=True)
            sum1 = jnp.sum(pull * offset, axis=0, keepdims=True)
            sum2 = jnp.sum(pull * square, axis=0, keepdims=True)
            d_centre = -sum1 / spread * centre * (1.0 - centre)
            d_spread = (sum2 / spread - sum0) * (0.5 * spread_var) / spread
            d_spread = d_spread / (1.0 + jnp.exp(-spread_arg))
            pulls += [d_centre, d_spread]
            dq_acc[lo:hi, here] = ut_ref[lo:hi, 0:1] * d_centre + ut_ref[lo:hi, 1:2] * d_spread
        stacked = jnp.concatenate(pulls + [jnp.zeros((4, rows), f32)], axis=0)
        high_part = stacked.astype(bf16)
        low_part = (stacked - high_part.astype(f32)).astype(bf16)
        da_acc[...] += mm(high_part, q) + mm(low_part, q)
        return 0

    lax.fori_loop(0, count, mem_step, 0)
    dmv_ref[...] = dmv_acc[...].astype(bf16)
    row8 = lax.broadcasted_iota(jnp.int32, (8, LANES), 0)
    da = da_acc[...]
    mu_row = jnp.where(inside[0], da[0:1, :], da[2:3, :])
    sig_row = jnp.where(inside[0], da[1:2, :], da[3:4, :])
    da_ref[...] = jnp.where(row8 == 0, mu_row, sig_row)

    def pull_tile(dk, dv, ks, vs, kat, qat, here, size_k, size_q, masked):
        q = q_ref[pl.ds(qat, size_q), :]
        g = g_ref[pl.ds(qat, size_q), :]
        for a in range(2):
            lo, hi = a * head, (a + 1) * head
            s = mm(ks[a], q, NT)
            p = jnp.exp(s - lse_ref[0, a : a + 1, here])
            if masked:
                key_id = lax.broadcasted_iota(jnp.int32, s.shape, 0)
                p = jnp.where(lax.broadcasted_iota(jnp.int32, s.shape, 1) >= key_id, p, 0.0)
            ds = (p * (mm(vs[a], g, NT) - term[a : a + 1, here])).astype(bf16)
            dv = dv + mm(p.astype(bf16), g * sel[a])
            dk = dk + mm(ds, q * sel_scale[a])
            dq_acc[lo:hi, here] += mm(kt[lo:hi, pl.ds(kat, size_k)], ds)
        return dk, dv

    def k_step(j, _):
        at = pl.multiple_of(order[j] * rows, rows)
        k = k_ref[pl.ds(at, rows), :]
        v = v_ref[pl.ds(at, rows), :]
        ks = [k * s for s in sel_scale]
        vs = [v * s for s in sel]
        zero = jnp.zeros((half, LANES), f32)
        here = pl.multiple_of(j * rows, rows)
        early = pull_tile(
            zero, zero, [x[:half] for x in ks], [x[:half] for x in vs], at, at,
            pl.ds(here, rows), half, rows, True
        )
        at_late = pl.multiple_of(at + half, half)
        late = pull_tile(
            zero, zero, [x[half:] for x in ks], [x[half:] for x in vs], at_late, at_late,
            pl.ds(pl.multiple_of(here + half, half), half), half, half, True
        )
        carry = tuple(jnp.concatenate([x, y], axis=0) for x, y in zip(early, late))

        def tile(i, carry):
            qat = pl.multiple_of(order[i] * rows, rows)
            there = pl.ds(pl.multiple_of(i * rows, rows), rows)
            return pull_tile(carry[0], carry[1], ks, vs, at, qat, there, rows, rows, False)

        dk, dv = lax.fori_loop(j + 1, count, tile, carry)
        dqkv_ref[1, pl.ds(at, rows), :] = dk.astype(bf16)
        dqkv_ref[2, pl.ds(at, rows), :] = dv.astype(bf16)
        return 0

    lax.fori_loop(0, count, k_step, 0)

    def q_out(i, _):
        at = pl.multiple_of(order[i] * rows, rows)
        here = pl.ds(pl.multiple_of(i * rows, rows), rows)
        dqkv_ref[0, pl.ds(at, rows), :] = dq_acc[:, here].T.astype(bf16)
        return 0

    lax.fori_loop(0, count, q_out, 0)


def attend_segment(projected, mem_kv, u_cols, order, flag, count, head):
    total_rows = projected.shape[0]
    width = projected.shape[1] // 3
    basis = mem_kv.shape[0]
    pairs = width // LANES
    rows = total_rows // count
    scale = 1.0 / math.sqrt(head)

    def column(base):
        return pl.BlockSpec((total_rows, LANES), lambda h, *_: (0, base + h))

    tiles = total_rows * (total_rows + rows) // 2 * 2 * pairs
    return pl.pallas_call(
        partial(forward_kernel, rows=rows, count=count, head=head, scale=scale),
        grid_spec=pltpu.PrefetchScalarGridSpec(
            num_scalar_prefetch=2,
            grid=(pairs,),
            in_specs=[
                column(0),
                column(pairs),
                column(2 * pairs),
                pl.BlockSpec((basis, LANES), lambda h, *_: (0, pairs + h)),
                pl.BlockSpec((LANES, 8), lambda h, *_: (h, 0)),
            ],
            out_specs=[
                column(0),
                column(0),
                pl.BlockSpec((1, 2, total_rows), lambda h, *_: (h, 0, 0)),
            ],
            scratch_shapes=[pltpu.VMEM((2, LANES, total_rows), bf16)],
        ),
        out_shape=[
            jax.ShapeDtypeStruct((total_rows, width), bf16),
            jax.ShapeDtypeStruct((total_rows, width), f32),
            jax.ShapeDtypeStruct((pairs, 2, total_rows), f32),
        ],
        compiler_params=pltpu.CompilerParams(vmem_limit_bytes=48 * 2**20),
        cost_estimate=pl.CostEstimate(
            flops=tiles * 4 * 256, transcendentals=tiles, bytes_accessed=12 * total_rows * width
        ),
        name="attend_forward",
    )(order, flag, projected, projected, projected, mem_kv, u_cols)


def attend_back(pair, kept, projected, mem_kv, u_cols, context_grad, local, lse, order, flag, count, head, mark, needs):
    total_rows = projected.shape[0]
    width = projected.shape[1] // 3
    basis = mem_kv.shape[0]
    pairs = width // LANES
    rows = total_rows // count
    scale = 1.0 / math.sqrt(head)

    def column(base):
        return pl.BlockSpec((total_rows, LANES), lambda h, *_: (0, base + pair))

    tiles = total_rows * (total_rows + rows) // 2 * 2
    kept = list(kept) if kept is not None else []
    extra = kept + [mark] + list(needs)
    outputs = pl.pallas_call(
        partial(backward_kernel, rows=rows, count=count, head=head, scale=scale, skip=len(extra)),
        grid_spec=pltpu.PrefetchScalarGridSpec(
            num_scalar_prefetch=2,
            grid=(1,),
            in_specs=[
                column(0),
                column(pairs),
                column(2 * pairs),
                pl.BlockSpec((basis, LANES), lambda h, *_: (0, pairs + pair)),
                pl.BlockSpec((LANES, 8), lambda h, *_: (pair, 0)),
                column(0),
                column(0),
                pl.BlockSpec((1, 2, total_rows), lambda h, *_: (pair, 0, 0)),
            ]
            + [pl.BlockSpec(memory_space=pl.ANY)] * len(extra),
            out_specs=[
                pl.BlockSpec((3, total_rows, LANES), lambda h, *_: (0, 0, pair)),
                pl.BlockSpec((basis, LANES), lambda h, *_: (0, pair)),
                pl.BlockSpec((8, LANES), lambda h, *_: (0, pair)),
            ]
            + [pl.BlockSpec(memory_space=pl.ANY)],
            scratch_shapes=[
                pltpu.VMEM((LANES, total_rows), f32),
                pltpu.VMEM((LANES, total_rows), bf16),
                pltpu.VMEM((8, total_rows), f32),
                pltpu.VMEM((basis, LANES), f32),
                pltpu.VMEM((8, LANES), f32),
            ],
        ),
        out_shape=[
            jax.ShapeDtypeStruct((3, total_rows, width), bf16),
            jax.ShapeDtypeStruct((basis, width), bf16),
            jax.ShapeDtypeStruct((8, width), f32),
        ]
        + [jax.ShapeDtypeStruct(mark.shape, mark.dtype)],
        input_output_aliases={10 + c: c + 3 - len(kept) for c in range(len(kept) + 1)},
        compiler_params=pltpu.CompilerParams(vmem_limit_bytes=48 * 2**20),
        cost_estimate=pl.CostEstimate(
            flops=tiles * 10 * 256, transcendentals=tiles, bytes_accessed=20 * total_rows * LANES
        ),
        name=f"attend_backward_{pair}",
    )(
        order, flag, projected, projected, projected, mem_kv, u_cols, context_grad, local, lse, *extra
    )
    return outputs[:3], outputs[3]


def row_stats(values):
    centred = values - jnp.mean(values, axis=-1, keepdims=True)
    inverse = lax.rsqrt(jnp.mean(centred * centred, axis=-1, keepdims=True) + eps_norm)
    return centred * inverse, inverse


def pull_norm(upstream, unit_rows, inverse, gain_vec):
    scaled = upstream * gain_vec
    return inverse * (
        scaled
        - jnp.mean(scaled, axis=-1, keepdims=True)
        - unit_rows * jnp.mean(scaled * unit_rows, axis=-1, keepdims=True)
    )


def front_kernel(pos, x_ref, gain, bias, w_ref, high_ref, low_ref, *refs, kept):
    copy_ref, normed_ref, proj_ref, sum_ref = refs[-4:]
    copy_ref[...] = x_ref[...]
    unit, _ = row_stats(x_ref[...].astype(f32))
    normed = (unit * gain[...] + bias[...]).astype(bf16)
    normed_ref[...] = normed
    width = normed.shape[1]
    for c in range(3):
        cols = slice(c * width, (c + 1) * width)
        proj_ref[:, cols] = mm(normed, w_ref[:, cols]).astype(bf16)

    @pl.when(pl.program_id(0) == 0)
    def _():
        sum_ref[...] = refs[0][...] if kept else jnp.zeros_like(sum_ref)

    sum_ref[...] += mm(high_ref[...], normed) + mm(low_ref[...], normed)


def front(inputs, base, total_rows, kept, gain, bias, w_qkv, tables, slot_pos, rows):
    width = inputs.shape[1]
    basis = tables[0].shape[0]
    count = inputs.shape[0] // rows
    whole = lambda shape: pl.BlockSpec(shape, lambda i, pos: (0, 0), pipeline_mode=pl.Buffered(1))
    ridge = pl.BlockSpec((basis, rows), lambda i, pos: (0, pos[base + i]))
    block = pl.BlockSpec((rows, width), lambda i, pos: (base + i, 0))
    kept = list(kept[3:]) + list(kept[:3]) if kept is not None else []
    kept_specs = [whole((basis, width))] + [pl.BlockSpec(memory_space=pl.ANY)] * 3 if kept else []
    return pl.pallas_call(
        partial(front_kernel, kept=bool(kept)),
        grid_spec=pltpu.PrefetchScalarGridSpec(
            num_scalar_prefetch=1,
            grid=(count,),
            in_specs=[
                pl.BlockSpec((rows, width), lambda i, pos: (i, 0)),
                whole((1, width)),
                whole((1, width)),
                whole(w_qkv.shape),
                ridge,
                ridge,
            ]
            + kept_specs,
            out_specs=[
                block,
                block,
                pl.BlockSpec((rows, 3 * width), lambda i, pos: (base + i, 0)),
                pl.BlockSpec((basis, width), lambda i, pos: (0, 0)),
            ],
        ),
        out_shape=[
            jax.ShapeDtypeStruct((total_rows, width), bf16),
            jax.ShapeDtypeStruct((total_rows, width), bf16),
            jax.ShapeDtypeStruct((total_rows, 3 * width), bf16),
            jax.ShapeDtypeStruct((basis, width), f32),
        ],
        input_output_aliases={8 + c: c for c in range(3)} if kept else {},
        compiler_params=pltpu.CompilerParams(vmem_limit_bytes=40 * 2**20),
        cost_estimate=pl.CostEstimate(
            flops=2 * count * rows * width * (3 * width + 2 * basis),
            transcendentals=0,
            bytes_accessed=10 * count * rows * width + 2 * w_qkv.size,
        ),
        name=f"front_{base}",
    )(slot_pos, inputs, gain[None], bias[None], w_qkv, *tables, *kept)


gelu_in = math.sqrt(2.0 / math.pi)
gelu_cube = 0.044715


def middle_kernel(
    core, x_ref, att_ref, go_ref, gain, bias, w_out, w_fc, w_proj,
    res_ref, mid_ref, ctx_ref, d_keep, d_send, d_vec, out_acc, fc_acc, proj_acc, *, blocks, parts
):
    step = pl.program_id(0)
    width = x_ref.shape[1]

    @pl.when(step == 0)
    def _():
        out_acc[...] = jnp.zeros_like(out_acc)
        fc_acc[...] = jnp.zeros_like(fc_acc)
        proj_acc[...] = jnp.zeros_like(proj_acc)
        d_vec[...] = jnp.zeros_like(d_vec)

    @pl.when(step < blocks)
    def _():
        att = att_ref[...]
        go = go_ref[...]
        middle = x_ref[...].astype(f32) + mm(att, w_out[...])
        unit, inverse = row_stats(middle)
        second = (unit * gain[...] + bias[...]).astype(bf16)
        res = middle
        back = jnp.zeros_like(middle)
        chunk = w_fc.shape[1] // parts
        for c in range(parts):
            cols = slice(c * chunk, (c + 1) * chunk)
            pre = mm(second, w_fc[:, cols])
            square = pre * pre
            t = jnp.tanh(gelu_in * pre * (1.0 + gelu_cube * square))
            rise = 0.5 * (1.0 + t)
            hidden = (pre * rise).astype(bf16)
            slope = rise + pre * (1.0 - t * t) * (0.5 * gelu_in + (1.5 * gelu_in * gelu_cube) * square)
            res = res + mm(hidden, w_proj[cols, :])
            pre_grad = (mm(go, w_proj[cols, :], NT) * slope).astype(bf16)
            back = back + mm(pre_grad, w_fc[:, cols], NT)
            proj_acc[c] += mm(hidden, go, TN)
            fc_acc[c] += mm(second, pre_grad, TN)
        res_ref[...] = res.astype(bf16)
        d_vec[0:1, :] += jnp.sum(back * unit, axis=0, keepdims=True)
        d_vec[1:2, :] += jnp.sum(back, axis=0, keepdims=True)
        mid_grad = go.astype(f32) + pull_norm(back, unit, inverse, gain[...])
        mid_ref[...] = mid_grad
        branch = mid_grad.astype(bf16)
        ctx_ref[...] = mm(branch, w_out[...], NT).astype(bf16)
        out_acc[...] += mm(att, branch, TN).reshape(out_acc.shape)

    def leave(ref):
        chunk = proj_acc.shape[1]
        part = lax.rem(step - blocks + core[0] * (parts // 2), parts)
        ref[:width, :] = fc_acc[part].astype(bf16)
        ref[width : width + chunk, :] = proj_acc[part].astype(bf16)
        ref[width + chunk :, :] = out_acc[part].astype(bf16)

    @pl.when((step >= blocks) & (step < blocks + parts // 2))
    def _():
        leave(d_keep)

    @pl.when(step >= blocks + parts // 2)
    def _():
        leave(d_send)


def middle_rows(core, inputs, attended, out_rows, gain, bias, w_out, w_fc, w_proj, rows):
    total_rows, width = inputs.shape
    hidden = w_fc.shape[1]
    blocks = total_rows // rows
    parts = hidden // width
    chunk, share = hidden // parts, width // parts
    whole = lambda shape: pl.BlockSpec(shape, lambda i, core: (0, 0), pipeline_mode=pl.Buffered(1))
    block = pl.BlockSpec((rows, width), lambda i, core: (jnp.minimum(i, blocks - 1), 0))
    half = parts // 2
    leaving = lambda base: pl.BlockSpec(
        (width + chunk + share, width), lambda i, core: (jnp.clip(i - blocks - base, 0, half - 1), 0)
    )
    macs = total_rows * width * (6 * hidden + 3 * width)
    return pl.pallas_call(
        partial(middle_kernel, blocks=blocks, parts=parts),
        grid_spec=pltpu.PrefetchScalarGridSpec(
            num_scalar_prefetch=1,
            grid=(blocks + parts,),
            in_specs=[
            block,
            block,
            block,
            whole((1, width)),
            whole((1, width)),
            whole(w_out.shape),
            whole(w_fc.shape),
            whole(w_proj.shape),
        ],
        out_specs=[
            block,
            block,
            block,
            leaving(0),
            leaving(half),
            pl.BlockSpec((8, width), lambda i, core: (0, 0)),
        ],
        scratch_shapes=[
            pltpu.VMEM((parts, share, width), f32),
            pltpu.VMEM((parts, width, chunk), f32),
            pltpu.VMEM((parts, chunk, width), f32),
        ],
        ),
        out_shape=[
            jax.ShapeDtypeStruct((total_rows, width), bf16),
            jax.ShapeDtypeStruct((total_rows, width), f32),
            jax.ShapeDtypeStruct((total_rows, width), bf16),
            jax.ShapeDtypeStruct((half * (width + chunk + share), width), bf16),
            jax.ShapeDtypeStruct((half * (width + chunk + share), width), bf16),
            jax.ShapeDtypeStruct((8, width), f32),
        ],
        compiler_params=pltpu.CompilerParams(vmem_limit_bytes=60 * 2**20),
        cost_estimate=pl.CostEstimate(
            flops=2 * macs, transcendentals=total_rows * hidden, bytes_accessed=60 * 2**20
        ),
        name="middle_rows",
    )(core, inputs, attended, out_rows, gain[None], bias[None], w_out, w_fc, w_proj)


def last_kernel(
    pos, x_ref, mid_ref, d_ref, gain, w_ref, cot_ref, high_ref, low_ref, vec_ref, *refs
):
    out_ref, d_vec = refs[-3:-1]
    @pl.when(pl.program_id(0) == 0)
    def _():
        d_vec[...] = vec_ref[...]

    width = x_ref.shape[1]
    up = mm(high_ref[...], cot_ref[...]) + mm(low_ref[...], cot_ref[...])
    for c in range(3):
        up = up + mm(d_ref[c], w_ref[:, c * width : (c + 1) * width], NT)
    unit, inverse = row_stats(x_ref[...].astype(f32))
    d_vec[0:1, :] += jnp.sum(up * unit, axis=0, keepdims=True)
    d_vec[1:2, :] += jnp.sum(up, axis=0, keepdims=True)
    out_ref[...] = (mid_ref[...] + pull_norm(up, unit, inverse, gain[...])).astype(bf16)


def last_rows(
    base, count, inputs, middle_grad, dqkv, gain, w_qkv, mem_cot, tables, slot_pos, rows, vectors, mark, needs
):
    width = inputs.shape[1]
    basis = tables[0].shape[1]
    whole = lambda shape: pl.BlockSpec(shape, lambda i, pos: (0, 0), pipeline_mode=pl.Buffered(1))
    block = pl.BlockSpec((rows, width), lambda i, pos: (base + i, 0))
    ridge = pl.BlockSpec((rows, basis), lambda i, pos: (pos[base + i], 0))
    anywhere = pl.BlockSpec(memory_space=pl.ANY)
    return pl.pallas_call(
        last_kernel,
        grid_spec=pltpu.PrefetchScalarGridSpec(
            num_scalar_prefetch=1,
            grid=(count,),
            in_specs=[
                block,
                block,
                pl.BlockSpec((3, rows, width), lambda i, pos: (0, base + i, 0)),
                whole((1, width)),
                whole(w_qkv.shape),
                whole(mem_cot.shape),
                ridge,
                ridge,
                whole(vectors.shape),
                anywhere,
            ]
            + [anywhere] * len(needs),
            out_specs=[
                pl.BlockSpec((rows, width), lambda i, pos: (i, 0)),
                pl.BlockSpec((8, width), lambda i, pos: (0, 0)),
                anywhere,
            ],
        ),
        out_shape=[
            jax.ShapeDtypeStruct((count * rows, width), bf16),
            jax.ShapeDtypeStruct((8, width), f32),
            jax.ShapeDtypeStruct(mark.shape, mark.dtype),
        ],
        input_output_aliases={10: 2},
        compiler_params=pltpu.CompilerParams(vmem_limit_bytes=40 * 2**20),
        cost_estimate=pl.CostEstimate(
            flops=2 * count * rows * width * (3 * width + 2 * basis),
            transcendentals=0,
            bytes_accessed=16 * count * rows * width + 2 * w_qkv.size,
        ),
        name=f"last_rows_{base}",
    )(slot_pos, inputs, middle_grad, dqkv, gain[None], w_qkv, mem_cot, *tables, vectors, mark, *needs)


def density_of(queries, u_mu, u_sig, basis_count):
    highest = lax.Precision.HIGHEST
    centres = (jnp.arange(basis_count, dtype=f32) + 0.5) / basis_count
    width_b = 0.75 / basis_count
    wide = queries.astype(f32)
    centre = jax.nn.sigmoid(jnp.einsum("qhd,hd->qh", wide, u_mu, precision=highest))
    spread = spread_var * jax.nn.softplus(
        jnp.einsum("qhd,hd->qh", wide, u_sig, precision=highest)
    )
    spread = (spread + spread_floor)[..., None]
    offset = centre[..., None] - centres
    return width_b * lax.rsqrt(spread) * jnp.exp(-offset * offset / (2.0 * spread))


def spread_attend(projected, mem_kv, u_mu, u_sig, q_pos, k_pos, team, flag, heads):
    rows, width = projected.shape[0], projected.shape[1] // 3
    basis = mem_kv.shape[0]
    head = width // heads
    scale = 1.0 / math.sqrt(head)
    shape = (-1, heads, head)
    queries = projected[:, :width].reshape(shape)
    both = lax.all_gather(projected[:, width:], "blk", axis=0, tiled=True, axis_index_groups=team)
    keys, values = both[:, :width].reshape(shape), both[:, width:].reshape(shape)
    scores = jnp.einsum("qhd,khd->hqk", queries, keys, preferred_element_type=f32) * scale
    allowed = (q_pos[:, None] >= k_pos[None, :])[None]
    scores = jnp.where(allowed, scores, masked_value)
    lse = jax.nn.logsumexp(scores, axis=-1, keepdims=True)
    probs = jnp.where(allowed, jnp.exp(scores - lse), 0.0)
    local = jnp.einsum("hqk,khd->qhd", probs.astype(bf16), values, preferred_element_type=f32)
    mem_values = mem_kv[:, width:].reshape(shape)
    density = density_of(queries, u_mu, u_sig, basis).astype(bf16)
    mem = jnp.einsum("qhn,nhd->qhd", density, mem_values, preferred_element_type=f32)
    attended = (local + flag.astype(f32) * mem).astype(bf16).reshape(rows, width)
    return attended, (queries, keys, values, probs, local, density, mem_values)


def spread_back(kept, context_grad, u_mu, u_sig, team, flag):
    queries, keys, values, probs, local, density, mem_values = kept
    rows, heads, head = queries.shape
    basis = mem_values.shape[0]
    scale = 1.0 / math.sqrt(head)
    g = context_grad.reshape(queries.shape)
    term = jnp.sum(g.astype(f32) * local, axis=-1)
    dv = jnp.einsum("hqk,qhd->khd", probs.astype(bf16), g, preferred_element_type=f32)
    dp = jnp.einsum("qhd,khd->hqk", g, values, preferred_element_type=f32)
    ds = (probs * (dp - term.T[..., None])).astype(bf16)
    dq = jnp.einsum("hqk,khd->qhd", ds, keys, preferred_element_type=f32) * scale
    dk = jnp.einsum("hqk,qhd->khd", ds, queries, preferred_element_type=f32) * scale
    both = jnp.stack([dk.reshape(-1, heads * head), dv.reshape(-1, heads * head)], 1).astype(bf16)
    both = lax.psum_scatter(both, "blk", scatter_dimension=0, tiled=True, axis_index_groups=team)
    g_on = g * flag.astype(bf16)
    pull = jnp.einsum("qhd,nhd->qhn", g_on, mem_values, preferred_element_type=f32)
    dmv = jnp.einsum("qhn,qhd->nhd", density, g_on, preferred_element_type=f32)
    dq_mem, d_mu, d_sig = jax.vjp(
        lambda q, m, s: density_of(q, m, s, basis), queries.astype(f32), u_mu, u_sig
    )[1](pull)
    dqkv = jnp.stack([(dq + dq_mem).reshape(rows, -1).astype(bf16), both[:, 0], both[:, 1]])
    return dqkv, dmv.reshape(basis, -1), d_mu.reshape(1, -1), d_sig.reshape(1, -1)


def per_device(
    tokens,
    memory,
    present,
    block_pos,
    ln1_gain,
    ln1_bias,
    w_qkv,
    w_out,
    ln2_gain,
    ln2_bias,
    w_fc,
    w_proj,
    w_mu,
    w_sig,
    grad_out,
    grad_memory,
):
    members, seg_rows, model_width = tokens.shape
    blocks = lax.axis_size("blk")
    teams = blocks // members
    heads, basis = w_mu.shape
    head = model_width // heads
    total_rows = members * seg_rows
    seg_len = seg_rows * blocks
    scale = 1.0 / math.sqrt(head)
    rank = lax.axis_index("blk")
    member, team_rank = rank % members, rank // members
    team = [[s + members * j for j in range(teams)] for s in range(members)]

    token_slots = collect_blocks(tokens, members)
    token_slots, grad_out = lax.optimization_barrier((token_slots, grad_out))
    grad_slots = collect_blocks(grad_out, members)
    mem = pick(memory, member)
    mem_cot = pick(grad_memory, member)
    flag = lax.dynamic_slice_in_dim(present, member, 1, 0)
    on = flag[0].astype(f32)
    seg_order = pick(block_pos, member)
    back = source_of(member, jnp.arange(members, dtype=jnp.int32), members)
    slot_pos = seg_order[team_rank * members + back]

    ridge_table, carry_table = memory_tables(basis, seg_len)
    ridge_parts = [jnp.asarray(part) for part in split_low(ridge_table)]
    ridge_turned = [jnp.asarray(part) for part in split_low(ridge_table.T)]
    carry_parts = [jnp.asarray(part) for part in split_low(carry_table)]

    begun = None
    near_slots = near(members)
    for first, last in ((0, near_slots), (near_slots, members)):
        if first < last:
            begun = front(
                jnp.concatenate(token_slots[first:last], axis=0), first, total_rows, begun,
                ln1_gain, ln1_bias, w_qkv, ridge_parts, slot_pos, seg_rows,
            )
    inputs_low, normed_low, projected, gathered = begun
    mem_kv = mm(mem, w_qkv[:, model_width:]).astype(bf16)
    mem_keys = mem_kv[:, :model_width].astype(f32)
    wide_mu = jnp.repeat(w_mu.T, head, axis=1)
    wide_sig = jnp.repeat(w_sig.T, head, axis=1)
    u_mu = scale * jnp.sum(mem_keys * wide_mu, axis=0)
    u_sig = scale * jnp.sum(mem_keys * wide_sig, axis=0)

    if teams > 1:
        gathered = lax.psum(gathered, "blk", axis_index_groups=team)
    new_memory = (on * sum(mm(part, mem) for part in carry_parts) + gathered).astype(bf16)

    if teams == 1:
        order = jnp.argmax(
            slot_pos[None, :] == jnp.arange(members, dtype=jnp.int32)[:, None], axis=1
        ).astype(jnp.int32)
        u_cols = jnp.concatenate(
            [u_mu[:, None], u_sig[:, None], jnp.zeros((model_width, 6), f32)], axis=1
        )
        attended, local, lse = attend_segment(projected, mem_kv, u_cols, order, flag, members, head)
    else:
        row_ids = jnp.arange(seg_rows, dtype=jnp.int32)
        q_pos = (slot_pos[:, None] * seg_rows + row_ids[None, :]).reshape(-1)
        key_order = seg_order.reshape(teams, members)[:, back]
        k_pos = (key_order[:, :, None] * seg_rows + row_ids).reshape(-1)
        mu_heads, sig_heads = u_mu.reshape(heads, head), u_sig.reshape(heads, head)
        attended, kept = spread_attend(
            projected, mem_kv, mu_heads, sig_heads, q_pos, k_pos, team, flag, heads
        )
    new_memory = share_segments(new_memory, members)

    out_rows = jnp.concatenate(grad_slots, axis=0)
    result_rows, middle_grad, context_grad, d_keep, d_send, ln2_grads = middle_rows(
        (rank % near(blocks)).astype(jnp.int32)[None], inputs_low, attended, out_rows, ln2_gain, ln2_bias, w_out, w_fc, w_proj,
        min(256, total_rows),
    )
    slots = result_rows.reshape(members, seg_rows, model_width)
    near_slots = near(members)

    def qkv_part(first, last):
        cols = slice(first, last)
        parts = [mm(normed_low, dqkv[0, :, cols], TN)]
        parts.append(mm(normed_low, dqkv[1, :, cols], TN))
        parts.append(mm(normed_low, dqkv[2, :, cols], TN))
        mem_grads = (mem_keys_part(cols), mem_values_grad[:, cols])
        for c in range(2):
            parts[c + 1] = parts[c + 1] + mm(mem_once, mem_grads[c], TN)
        return jnp.concatenate([part.astype(bf16) for part in parts], axis=1)

    def mem_keys_part(cols):
        part = wide_mu[:, cols] * mu_sum[:, cols] + wide_sig[:, cols] * sig_sum[:, cols]
        return part.astype(bf16)

    mem_once = mem * (team_rank == 0).astype(bf16)
    pairs = model_width // LANES
    early = 2 * pairs // 3
    kept_back = None
    mark = jnp.zeros((8, LANES), jnp.int32)

    def stage(pair, needs):
        nonlocal kept_back, mark
        if teams == 1:
            kept_back, mark = attend_back(
                pair, kept_back, projected, mem_kv, u_cols, context_grad, local, lse, order, flag,
                members, head, mark, needs
            )
        return mark[0, 0]

    near_parts = [slots[0]] + [return_slot(slots, d, members) for d in range(1, near_slots)]
    terms = [d_keep] + send_whole(d_send, "core")
    zero = stage(0, [d_keep])
    middle_row = d_keep.shape[0] // 2
    own_a, got_a = send_parts([term[:middle_row] for term in terms], "x", zero)
    own_b, got_b = send_parts([term[middle_row:] for term in terms], "y", zero)
    zero = stage(1, [own_a, own_b])
    own_a, got_a = send_parts([own_a] + got_a, "y", zero)
    own_b, got_b = send_parts([own_b] + got_b, "x", zero)
    zero = stage(2, [own_a, own_b])
    count_a = own_a.shape[0]
    terms = [jnp.concatenate([own_a, own_b])]
    if len(got_a) == len(got_b):
        terms += [jnp.concatenate(both) for both in zip(got_a, got_b)]
    else:
        sum_a = sum(part.astype(f32) for part in got_a).astype(bf16)
        sum_b = sum(part.astype(f32) for part in got_b).astype(bf16)
        terms.append(jnp.concatenate([sum_a, sum_b]))
    own, got = send_parts(terms, "z", zero)
    far_parts = [return_slot(slots, d, members) for d in range(near_slots, members)]
    zero = stage(3, [own])
    mem_once = mem * (team_rank == 0).astype(bf16)
    if teams == 1:
        dqkv, mem_values_grad, pulls = kept_back
        mu_sum, sig_sum = scale * pulls[0:1], scale * pulls[1:2]
    else:
        dqkv, mem_values_grad, mu_part, sig_part = spread_back(
            kept, context_grad, mu_heads, sig_heads, team, flag
        )
        mu_part, sig_part = scale * mu_part, scale * sig_part
        mem_values_grad, mu_sum, sig_sum = lax.psum(
            (mem_values_grad, mu_part, sig_part), "blk", axis_index_groups=team
        )
        mem_values_grad = mem_values_grad.astype(bf16)
    own_e, got_e = send_parts([qkv_part(0, early * LANES)], "core")
    own = sum(term.astype(f32) for term in [own] + got) + zero.astype(f32)
    own = own.astype(bf16)
    got = send_whole(own, "z")
    result = place_blocks(near_parts + far_parts, members, zero)
    zero = stage(4, [own, new_memory, own_e, result])
    full = place(own, got, "z", zero)
    own_a, own_b = full[:count_a], full[count_a:]
    got_a, got_b = send_whole(own_a, "y"), send_whole(own_b, "x")
    own_e, got_e = send_parts([own_e] + got_e, "x", zero)
    zero = stage(5, [own_a, own_b, own_e])
    if teams == 1:
        dqkv, mem_values_grad, pulls = kept_back
        mu_sum, sig_sum = scale * pulls[0:1], scale * pulls[1:2]
        mu_part, sig_part = mu_sum, sig_sum
    own_a, own_b = place(own_a, got_a, "y", zero), place(own_b, got_b, "x", zero)
    got_a, got_b = send_whole(own_a, "x"), send_whole(own_b, "y")
    own_l, got_l = send_parts([qkv_part(early * LANES, model_width)], "core")
    ln1_grads = jnp.zeros((8, model_width), f32)
    back_parts = [None] * members
    for first, last in ((near_slots, members), (0, near_slots)):
        if first == last:
            continue
        token_grad, ln1_grads, mark = last_rows(
            first, last - first, inputs_low, middle_grad, dqkv, ln1_gain, w_qkv, mem_cot, ridge_turned,
            slot_pos, seg_rows, ln1_grads, mark,
            [own_a, own_b, own_e, own_l] if first == near_slots else [own_l] + got_a + got_b,
        )
        slots = {d: token_grad[(d - first) * seg_rows : (d - first + 1) * seg_rows] for d in range(first, last)}
        for d in range(first, last):
            back_parts[d] = slots[0] if d == 0 else return_slot(slots, d, members)
        if first == near_slots:
            own_l, got_l = send_parts([own_l] + got_l, "x", mark[0, 0])
    zero = mark[0, 0]
    terms = [jnp.concatenate(both, axis=1) for both in zip([own_e] + got_e, [own_l] + got_l)]
    own, got = send_parts(terms, "y", zero)
    own, got = send_parts([own] + got, "z")
    qkv_sum = sum(term.astype(f32) for term in [own] + got).astype(bf16)
    for name in ("z", "y", "x"):
        qkv_sum = place(qkv_sum, send_whole(qkv_sum, name), name)
    w_own = jnp.concatenate([place(own_a, got_a, "x", zero), place(own_b, got_b, "y", zero)])
    w_got = send_whole(w_own, "core")
    qkv_got = send_whole(qkv_sum, "core")
    grad_tokens = place_blocks(back_parts, members)

    mem_keys_grad = mem_keys_part(slice(None))
    w_mu_grad = jnp.sum((mem_keys * mu_part).reshape(basis, heads, head), axis=2).T
    w_sig_grad = jnp.sum((mem_keys * sig_part).reshape(basis, heads, head), axis=2).T
    memory_grad = (
        on
        * (
            mm(mem_keys_grad, w_qkv[:, model_width : 2 * model_width], NT)
            + mm(mem_values_grad, w_qkv[:, 2 * model_width :], NT)
            + sum(mm(part, mem_cot, TN) for part in carry_parts)
        )
    ).astype(bf16)
    memory_grad = share_segments(memory_grad, members)

    qkv_cols = place(qkv_sum, qkv_got, "core").astype(f32)
    split = early * LANES
    rest = model_width - split
    w_qkv_grad = jnp.concatenate(
        [
            piece
            for c in range(3)
            for piece in (
                qkv_cols[:, c * split : (c + 1) * split],
                qkv_cols[:, 3 * split + c * rest : 3 * split + (c + 1) * rest],
            )
        ],
        axis=1,
    )
    parts = w_fc.shape[1] // model_width
    pieces = place(w_own, w_got, "core").reshape(parts, -1, model_width).astype(f32)
    w_fc_grad = jnp.concatenate([pieces[c, :model_width] for c in range(parts)], axis=1)
    w_proj_grad = pieces[:, model_width : 2 * model_width].reshape(w_proj.shape)
    w_out_grad = pieces[:, 2 * model_width :].reshape(w_out.shape)

    vectors = jnp.concatenate(
        [ln1_grads[:2].reshape(-1), ln2_grads[:2].reshape(-1), w_mu_grad.reshape(-1), w_sig_grad.reshape(-1)]
    )
    vectors = sum_all(vectors.reshape(-1, LANES)).reshape(-1)
    ln1_gain_grad, ln1_bias_grad, ln2_gain_grad, ln2_bias_grad = [
        vectors[c * model_width : (c + 1) * model_width] for c in range(4)
    ]
    tail = vectors[4 * model_width :].reshape(2, heads, basis)
    w_mu_grad, w_sig_grad = tail[0], tail[1]
    return (
        result,
        new_memory,
        grad_tokens,
        memory_grad,
        ln1_gain_grad,
        ln1_bias_grad,
        w_qkv_grad,
        w_out_grad,
        ln2_gain_grad,
        ln2_bias_grad,
        w_fc_grad,
        w_proj_grad,
        w_mu_grad,
        w_sig_grad,
    )


def solution(mesh):
    split = P("seg", "blk", None)
    whole_seg = P("seg", None, None)
    return jax.shard_map(
        per_device,
        mesh=mesh,
        in_specs=(split, whole_seg, P("seg"), P("seg", None)) + (P(),) * 10 + (split, whole_seg),
        out_specs=(split, whole_seg, split, whole_seg) + (P(),) * 10,
        check_vma=False,
    )
```
